512 devices in a mesh: cube: 8 (over x, core), front: 64 (over z, y).
Axes of the slice: x: 4, y: 4, z: 16, core: 2. Of those that a mesh axis runs over, the one named last changes fastest.
Arguments:
- leaf_blocks: float32 [8, 3840, 3840], P('cube', 'front'), may hold values from -8 to 11, as said below
- front_entries: float32 [7, 4096, 256], P(None, 'front'), may hold values from -0.001 to 3
- child_maps: int32 [7, 2, 60], replicated, may hold values from 0 to 63, as said below
Outputs:
- factor_columns: float32 [8, 3, 4096, 256], P('cube', None, 'front')
- top_block: float32 [3840, 3840], P('front')
The draws below stay inside these ranges and needn't reach their ends.
Inputs may be any that keep to these rules, and one draw needn't show every extreme that they name: `child_maps`: for each node, each of the two rows lists distinct offsets, and the two rows together name every offset from 0 to 63. `leaf_blocks`: each leaf block is symmetric positive definite.
All inputs are finite; a program needn't handle non-finite values.
Results may differ from the reference program's by a relative error of at most 0.00033.
Values may be sent and summed in bfloat16 or wider, within the bound.
No kernel may reach another device: no remote copies, remote signals or barrier semaphores. Data moves between devices by JAX's collectives and lax.ppermute only.
A program may use at most 128 MiB of HBM per device.

```python
import jax
import jax.numpy as jnp
from jax import lax

FRONT = 4096
SEP = 256
PANEL = 256
CB = 3840
CUBES = 8
NODES = 7
LEVELS = 3
ROWS = 64
SEP_ROWS = 4
CB_ROWS = 60
N_CUBE = 8
N_FRONT = 64


def leaf_kernel(leaf_key):
    position_key, sign_key, scale_key, diag_key = jax.random.split(leaf_key, 4)
    extent = (CB / 7.5) ** (1.0 / 3.0)
    points = jax.random.uniform(position_key, (3, CB), jnp.float32, 0.0, extent)
    distance = jnp.zeros((CB, CB), jnp.float32)
    for axis_index in range(3):
        distance = distance + jnp.abs(points[axis_index][:, None] - points[axis_index][None, :])
    sign_values = 2.0 * jax.random.randint(sign_key, (CB,), 0, 2).astype(jnp.float32) - 1.0
    weights = jax.random.uniform(scale_key, (CB,), jnp.float32, 0.7, 1.3)
    signed = sign_values * weights
    kernel = 2.0 * signed[:, None] * signed[None, :] * jnp.exp(-distance)
    diag_extra = jax.random.uniform(diag_key, (CB,), jnp.float32, 2.0, 3.0)
    placed = jnp.arange(CB, dtype=jnp.int32)[:, None] == jnp.arange(CB, dtype=jnp.int32)[None, :]
    return kernel + jnp.where(placed, diag_extra[:, None], 0.0)


def draw_leaf_blocks(key, part):
    return lax.map(leaf_kernel, jax.random.split(key, CUBES))


def draw_front_entries(key, part):
    bound = 0.001
    noise = jax.random.uniform(key, (NODES, FRONT, SEP), jnp.float32, -bound, bound)
    diagonal = jax.random.uniform(jax.random.fold_in(key, 13), (NODES, FRONT, 1), jnp.float32, 1.0, 3.0)
    row_index = jnp.arange(FRONT, dtype=jnp.int32)[:, None]
    col_index = jnp.arange(SEP, dtype=jnp.int32)[None, :]
    placed = (row_index // ROWS == col_index // SEP_ROWS) & (row_index % ROWS == col_index % SEP_ROWS)
    return jnp.where(placed[None], diagonal, noise)


def draw_child_maps(key, part):

    def single(node_key):
        first_key, second_key, third_key = jax.random.split(node_key, 3)
        order = jax.random.permutation(first_key, ROWS).astype(jnp.int32)
        first_map = order[:CB_ROWS]
        missing = order[CB_ROWS:]
        picked = jax.random.permutation(second_key, first_map)[:CB_ROWS - SEP_ROWS]
        second_map = jax.random.permutation(third_key, jnp.concatenate([missing, picked]))
        return jnp.stack([first_map, second_map.astype(jnp.int32)])
    return jax.vmap(single)(jax.random.split(key, NODES))


def setup_inputs(seed: int = 0) -> dict:
    key_of = jax.random.split(jax.random.key(seed), 4)
    leaf_blocks = draw_leaf_blocks(jax.random.fold_in(key_of[3], 71), 0)
    front_entries = draw_front_entries(jax.random.fold_in(key_of[3], 71), 0)
    child_maps = draw_child_maps(jax.random.fold_in(key_of[3], 71), 0)
    return dict(leaf_blocks=leaf_blocks, front_entries=front_entries, child_maps=child_maps)


HIGH = lax.Precision.HIGHEST

def onehot_table(mapping, width):
    return (mapping[:, None] == jnp.arange(width, dtype=jnp.int32)[None, :]).astype(jnp.float32)

def scatter_block(block, mapping, devices, block_rows, width):
    table = onehot_table(mapping, width)
    grid = block.reshape(devices, block_rows, devices, block_rows)
    widened = jnp.einsum('aubv,vs->aubs', grid, table, precision=HIGH)
    return jnp.einsum('aubs,ut->atbs', widened, table, precision=HIGH)

def cholesky_lower(pivot):
    symmetric = jnp.tril(pivot) + jnp.tril(pivot, -1).T
    return jnp.linalg.cholesky(symmetric)

def eliminate(matrix, devices, width, sep_rows, panel_rows):
    panel = panel_rows * devices
    columns = []
    for index in range(sep_rows // panel_rows):
        first_row = index * panel_rows
        last_row = first_row + panel_rows
        trailing = width - last_row
        pivot = matrix[:, first_row:last_row, :, first_row:last_row]
        pivot = jnp.transpose(pivot, (1, 0, 3, 2)).reshape(panel, panel)
        factor = cholesky_lower(pivot)
        slab = matrix[:, last_row:, :, first_row:last_row]
        slab = jnp.transpose(slab, (0, 1, 3, 2)).reshape(devices * trailing, panel)
        solved = jax.scipy.linalg.solve_triangular(factor, slab.T, lower=True).T
        rounded = lax.optimization_barrier(solved.astype(jnp.bfloat16)).astype(jnp.float32)
        update = jnp.dot(rounded, rounded.T, precision=HIGH)
        matrix = matrix.at[:, last_row:, :, last_row:].add(-update.reshape(devices, trailing, devices, trailing))
        upper = jnp.zeros((devices, first_row, panel), jnp.float32)
        middle = jnp.transpose(factor.reshape(panel_rows, devices, panel), (1, 0, 2))
        lower_part = solved.reshape(devices, trailing, panel)
        columns.append(jnp.concatenate([upper, middle, lower_part], axis=1))
    return (jnp.concatenate(columns, axis=2), matrix)

def reference(leaf_blocks, front_entries, child_maps):
    devices = N_FRONT
    width = FRONT // devices
    sep_rows = SEP // devices
    block_rows = CB // devices
    panel_rows = PANEL // devices
    blocks = [leaf_blocks[leaf] for leaf in range(N_CUBE)]
    factors = []
    for height in range(LEVELS):
        count = N_CUBE >> height + 1
        fresh = []
        level_factors = []
        for offset in range(count):
            node = count + offset
            matrix = jnp.zeros((devices, width, devices, width), jnp.float32)
            entries = front_entries[node - 1].reshape(devices, width, devices, sep_rows)
            matrix = matrix.at[:, :, :, :sep_rows].set(entries)
            matrix = matrix + scatter_block(blocks[2 * offset], child_maps[node - 1, 0], devices, block_rows, width)
            matrix = matrix + scatter_block(blocks[2 * offset + 1], child_maps[node - 1, 1], devices, block_rows, width)
            factor_part, matrix = eliminate(matrix, devices, width, sep_rows, panel_rows)
            level_factors.append(factor_part.reshape(FRONT, SEP))
            fresh.append(matrix[:, sep_rows:, :, sep_rows:].reshape(CB, CB))
        blocks = fresh
        factors.append(jnp.stack([level_factors[leaf >> height + 1] for leaf in range(N_CUBE)]))
    return (jnp.stack(factors, axis=1), blocks[0])
```

```python
import functools

import jax
import jax.numpy as jnp
from jax import lax
from jax.experimental import pallas as pl
from jax.experimental.pallas import tpu as pltpu
from jax.sharding import PartitionSpec as P

F32 = jnp.float32
BF16 = jnp.bfloat16
HIGH = lax.Precision.HIGHEST

N = 64
Z, Y = 16, 4
WIDTH = 64
KEEP = 60
PAN = 256
BLK = 32

Z_GROUPS = [[Y * z + y for z in range(Z)] for y in range(Y)]
Y_GROUPS = [[Y * z + y for y in range(Y)] for z in range(Z)]
CORE_GROUPS = [[0, 1], [2, 3], [4, 5], [6, 7]]
X_GROUPS = [[0, 2, 4, 6], [1, 3, 5, 7]]

VMEM = pl.BlockSpec(memory_space=pltpu.VMEM)
SMEM = pl.BlockSpec(memory_space=pltpu.SMEM)


def iota(shape, dim):
    return lax.broadcasted_iota(jnp.int32, shape, dim)


def split3(x):
    high = x.astype(BF16)
    rest = x - high.astype(F32)
    mid = rest.astype(BF16)
    low = (rest - mid.astype(F32)).astype(BF16)
    return high, mid, low


def dot(a, b, dims):
    return lax.dot_general(a, b, (dims, ((), ())), preferred_element_type=F32)


NN = ((1,), (0,))
NT = ((1,), (1,))
TN = ((0,), (0,))


def onehot_rows(row):
    return (iota((WIDTH, WIDTH), 0) == row).astype(BF16)


def compose(a, b):
    return dot(a, b, NN).astype(BF16)


def tail_table():
    return (iota((WIDTH, WIDTH), 0) + 4 == iota((WIDTH, WIDTH), 1)).astype(BF16)


def unpack(packed):
    full = jnp.concatenate([packed, pltpu.roll(packed, 64, 1)], axis=0)
    return jnp.where(iota(full.shape, 1) < WIDTH, full, 0.0)


def factor(a_ref, width):
    for b in range(PAN // BLK):
        j0 = b * BLK
        lo = j0 // 128 * 128
        rows = a_ref[j0 : j0 + BLK, lo:width]
        rid = iota((BLK, 1), 0)
        for i in range(BLK):
            jl = j0 - lo + i
            col = rows[:, jl : jl + 1]
            inv = 1.0 / rows[i : i + 1, jl : jl + 1]
            scale = jnp.where(rid > i, col * inv, 0.0)
            rows = rows - scale * rows[i : i + 1, :]
        head = rows[:, 0:128]
        diag = jnp.sum(
            jnp.where(iota(head.shape, 1) == iota(head.shape, 0) + (j0 - lo), head, 0.0),
            axis=1,
            keepdims=True,
        )
        root = lax.rsqrt(diag)
        root = root * (1.5 - 0.5 * diag * root * root)
        rows = rows * root
        a_ref[j0 : j0 + BLK, lo:width] = rows
        r0 = j0 + BLK
        if r0 < PAN:
            nlo = r0 // 128 * 128
            h, m, l = split3(rows[:, nlo - lo :])
            n = PAN - nlo
            left = jnp.concatenate([h, h, m, h, l, m], axis=0)[:, :n]
            right = jnp.concatenate([h, m, h, l, h, m], axis=0)
            done = dot(left, right, TN)
            a_ref[r0:PAN, nlo:width] -= done[r0 - nlo :, :]


def own_columns(own, position):
    p = iota(own.shape, 0)
    t = iota(own.shape, 1)
    kept = jnp.where((t < 4) & (p > t * N + position), 0.0, own)
    return jnp.transpose(kept)[:WIDTH, :]


def rows_of(g_ref, part, first, count, out_ref):
    for r in range(count):
        for y in range(Y):
            for half in range(2):
                out_ref[half, pl.ds(r * N + y, Z, stride=Y), :] = g_ref[
                    part, y, pl.ds(half * 12 + first + r, Z, stride=24), :
                ]


def joined(r, first, last):
    return jnp.concatenate([r[0, first:last, :], r[1, first:last, :]], axis=1)


def symmetric(g):
    return jnp.where(iota(g.shape, 1) >= iota(g.shape, 0), jnp.transpose(g), g)


def leaf_kernel(sc, maps_s, maps_v, leaf, entries, e_ref, ent_ref, ta_ref, tb_ref, big, inv):
    cube = sc[3]

    @pl.loop(0, 72)
    def _(k):
        inv[k] = -1

    @pl.loop(0, KEEP)
    def _(v):
        a0 = maps_s[0, v]
        a1 = maps_s[1, a0]
        a2 = maps_s[2, jnp.maximum(a1, 0)]
        code = jnp.where(a0 < 4, a0, jnp.where(a1 < 4, 4 + a1, 8 + a2))
        inv[code] = v

    t0 = onehot_rows(maps_v[0:1, :])
    t1 = compose(onehot_rows(maps_v[1:2, :]), t0)
    t2 = compose(onehot_rows(maps_v[2:3, :]), t1)
    tt = compose(tail_table(), t2)
    table = jnp.concatenate([tt, tt, t0, t0, t1, t1, t2, t2], axis=0).astype(F32)
    table = jnp.transpose(table).astype(BF16)
    table = jnp.concatenate([table, table, table], axis=0)

    pad = jnp.zeros((WIDTH - KEEP, 256), F32)
    for j in range(3840 // 256):
        block = leaf[0, :, j * 256 : (j + 1) * 256]
        block = jnp.concatenate([block, pad], axis=0)
        parts = jnp.concatenate(split3(block), axis=0)
        turned = dot(parts, table, TN)
        for f in range(4):
            big[f, j * 256 : (j + 1) * 256, :] = turned[:, f * 128 : (f + 1) * 128]

    lane = iota((N, 128), 1)
    for h in range(3):
        for k in range(2):
            pieces = []
            for side in range(2):
                v = inv[h * 4 + side * 2 + k]
                got = big[1 + h, pl.ds(jnp.maximum(v, 0), N, stride=KEEP), :]
                pieces.append(jnp.where(v >= 0, got, 0.0))
            e_ref[h, k * N : (k + 1) * N, :] = jnp.where(lane < WIDTH, pieces[0], pieces[1])

    half_lane = iota((N // 2, 128), 1)
    for s in range(8):
        r = jnp.bitwise_xor(s, cube)
        slot = jnp.bitwise_and(r, 2) + jnp.right_shift(r, 2)
        for i in range(8):
            dst = pl.ds(slot * 256 + i, N // 2, stride=8)
            if s * 8 + i < KEEP:
                v = inv[12 + s * 8 + i]
                start = jnp.maximum(v, 0)
                low = big[0, pl.ds(start, N // 2, stride=KEEP), :]
                high = big[0, pl.ds(start + KEEP * N // 2, N // 2, stride=KEEP), :]
                got = jnp.where(v >= 0, jnp.where(half_lane < WIDTH, low, high), 0.0)
            else:
                got = jnp.zeros((N // 2, 128), F32)

            @pl.when(jnp.bitwise_and(r, 1) == 0)
            def _():
                ta_ref[dst, :] = got

            @pl.when(jnp.bitwise_and(r, 1) == 1)
            def _():
                tb_ref[dst, :] = got

    p = iota((PAN, PAN), 0)
    order = (iota((PAN, PAN), 1) == (p % N) * 4 + p // N).astype(BF16)
    for h in range(3):
        e = entries[sc[h]]
        e3 = split3(e)
        placed = dot(order, e3[0], NT) + dot(order, e3[1], NT) + dot(order, e3[2], NT)
        ent_ref[h] = jnp.concatenate([placed[:128], placed[128:]], axis=1)


def pick_kernel(sc, maps_v, e0, e12, ent, x_ref, send_ref):
    core = sc[5]
    pair = sc[6]
    x0 = e0[0, 0] + e0[1, 0] + ent[0]
    q = [e12[x] for x in range(4)]
    low, high = q[0] + q[1], q[2] + q[3]
    x1 = jnp.where(pair == 0, low[0], high[0]) + ent[1]
    x2 = low[1] + high[1] + ent[2]
    x_ref[0], x_ref[1], x_ref[2] = x0, x1, x2
    m1 = onehot_rows(maps_v[1:2, :])
    m2 = onehot_rows(maps_v[2:3, :])
    m21 = compose(m2, m1)
    eye = (iota((WIDTH, WIDTH), 0) == iota((WIDTH, WIDTH), 1)).astype(BF16)

    def first4(tables):
        four = [x.astype(F32)[:8] for x in tables]
        while len(four) < 3:
            four.append(jnp.zeros_like(four[0]))
        return jnp.concatenate(four, axis=0)

    zero = jnp.zeros((8, WIDTH), F32)
    s0 = jnp.where(core == 0, first4([eye, m1, m21]), 0.0)
    s1 = jnp.where(core == 1, first4([eye, m2]), 0.0)
    s2 = jnp.where(
        core == 1, jnp.concatenate([zero, zero, eye.astype(F32)[:8]], axis=0), 0.0
    )
    z = jnp.zeros((24, PAN), F32)
    for s, x in ((s0, x0), (s1, x1), (s2, x2)):
        full = jnp.concatenate([x, pltpu.roll(x, 64, 1)], axis=0)[:, :WIDTH]
        table = s.astype(BF16)
        h, m, l = split3(full)
        z = z + (dot(table, h, NT) + dot(table, m, NT) + dot(table, l, NT))
    rows = jnp.concatenate([z[0:4], z[8:12], z[16:20]], axis=0)
    rows = jnp.concatenate([rows[:, :128], rows[:, 128:]], axis=0)
    for k in range(Z):
        send_ref[k] = rows


def level0_kernel(sc, maps_v, g, x, f_ref, v_ref, a, r):
    rows_of(g, 0, 0, 12, r)
    a[:, 0:256] = symmetric(joined(r, 0, 256))
    a[:, 256:768] = jnp.transpose(joined(r, 256, 768))
    a[:, 768:896] = unpack(x[0])
    factor(a, 896)
    own = a[:, 768:896]
    f_ref[...] = own_columns(own, sc[4])
    m1 = onehot_rows(maps_v[1:2, :])
    v_ref[:, 0:512] = a[:, 256:768].astype(BF16)
    moved = dot(own[:, :WIDTH].astype(BF16), m1, NT)
    v_ref[:, 512:640] = jnp.concatenate([moved, jnp.zeros_like(moved)], axis=1).astype(BF16)


def level1_kernel(sc, maps_v, g, x, v0, v0s, f_ref, d_ref, w_ref, dh_ref, wh_ref, a, r):
    rows_of(g, 1, 0, 8, r)
    a[:, 0:256] = symmetric(joined(r, 0, 256))
    a[:, 256:512] = jnp.transpose(joined(r, 256, 512))
    a[:, 512:640] = unpack(x[1])
    mine, other = v0[...], v0s[...]
    a[...] -= dot(mine[:, 0:256], mine, TN) + dot(other[:, 0:256], other, TN)
    factor(a, 640)
    own = a[:, 512:640]
    f_ref[...] = own_columns(own, sc[4])
    m2 = onehot_rows(maps_v[2:3, :])
    moved = [
        dot(mine[:, 512 : 512 + WIDTH], m2, NT).astype(BF16),
        dot(other[:, 512 : 512 + WIDTH], m2, NT).astype(BF16),
        dot(own[:, :WIDTH].astype(BF16), m2, NT).astype(BF16),
    ]
    cols = [mine[:, 256:512], other[:, 256:512], a[:, 256:512].astype(BF16)]
    zero = jnp.zeros((PAN, WIDTH), F32)
    w = jnp.concatenate([m.astype(F32) for m in moved] + [zero], axis=1).astype(BF16)
    w_ref[...] = w
    total = jnp.zeros((PAN, 384), F32)
    for c, m in zip(cols, moved):
        right = jnp.concatenate(
            [c.astype(F32), m.astype(F32), zero], axis=1
        ).astype(BF16)
        total = total + dot(c, right, TN)
    d_ref[...] = total
    first = pl.multiple_of(sc[5] * 128, 128)
    dh_ref[...] = d_ref[pl.ds(first, 128), :]
    wh_ref[...] = w_ref[pl.ds(first, 128), :]


def level2_kernel(sc, g, x, d, ds, w, ws, f_ref, send_ref, vw_ref, a, r):
    rows_of(g, 1, 8, 4, r)
    sib = jnp.concatenate([ds[0], ds[1]], axis=0)
    sub = d[...] + sib
    a[:, 0:256] = symmetric(joined(r, 0, 256)) - sub[:, 0:256]
    a[:, 256:384] = unpack(x[2]) - sub[:, 256:384]
    factor(a, 384)
    own = a[:, 256:384]
    f_ref[...] = own_columns(own, sc[4])
    wsib = jnp.concatenate([ws[0], ws[1]], axis=0)
    mine = w[...]
    pieces = [mine[:, n * WIDTH : (n + 1) * WIDTH] for n in range(3)]
    pieces += [wsib[:, n * WIDTH : (n + 1) * WIDTH] for n in range(3)]
    pieces.append(own[:, :WIDTH].astype(BF16))
    first = 4 + 8 * sc[3]
    pick = (iota((8, WIDTH), 0) + first == iota((8, WIDTH), 1)).astype(BF16)
    thick = jnp.concatenate([dot(pick, v, NT) for v in pieces], axis=0)
    thick = jnp.concatenate([thick[:, :128], thick[:, 128:]], axis=0).astype(BF16)
    for k in range(Z):
        send_ref[k] = thick
    src = iota((WIDTH, 128), 0)
    dst = iota((WIDTH, 128), 1)
    low = (src == dst + 4).astype(BF16)
    low = jnp.where(dst < KEEP, low, jnp.zeros_like(low))
    high = ((src == dst - 60) & (dst >= WIDTH)).astype(BF16)
    for n, v in enumerate(pieces):
        vw_ref[0, n * PAN : (n + 1) * PAN, :] = dot(v, low, NN).astype(BF16)
        vw_ref[1, n * PAN : (n + 1) * PAN, :] = dot(v, high, NN).astype(BF16)


def top_kernel(t_raw, got, vw, out, big):
    for y in range(Y):
        for z in range(Z):
            block = got[y, z].astype(F32)
            d = z * Y + y
            for n in range(7):
                for half in range(2):
                    first = half * 56 + n * 8
                    big[d * 8 : d * 8 + 8, (n * 2 + half) * 128 : (n * 2 + half + 1) * 128] = (
                        block[first : first + 8, :]
                    )
    low = dot(big[0:256, :].astype(BF16), vw[0], NN)
    high = dot(big[256:512, :].astype(BF16), vw[1], NN)
    out[...] = t_raw[...] - (low + high)


def last_kernel(t, out):
    for d in range(N // 2):
        block = jnp.concatenate([t[s, d * 8 : d * 8 + 8, :] for s in range(8)], axis=0)
        turned = jnp.transpose(block)
        out[:, d * KEEP : (d + 1) * KEEP] = turned[0:KEEP, 0:KEEP]
        d2 = d + N // 2
        out[:, d2 * KEEP : (d2 + 1) * KEEP] = turned[WIDTH : WIDTH + KEEP, 0:KEEP]


def call(kernel, specs, outs, scratch=(), flops=10**8, name=None):
    return pl.pallas_call(
        kernel,
        in_specs=specs,
        out_specs=[VMEM] * len(outs),
        out_shape=[jax.ShapeDtypeStruct(s, t) for s, t in outs],
        scratch_shapes=list(scratch),
        compiler_params=pltpu.CompilerParams(vmem_limit_bytes=48 * 2**20),
        cost_estimate=pl.CostEstimate(flops=flops, bytes_accessed=4 * 10**6, transcendentals=0),
        name=name,
    )


def crossed(value, mask):
    return lax.ppermute(value, "cube", [(c, c ^ mask) for c in range(8)])


def spread(value, axis_groups):
    return lax.all_to_all(value, "front", 0, 0, axis_index_groups=axis_groups, tiled=True)


def gather_front(sent, rows):
    lanes = sent.shape[-1]
    got = spread(sent.reshape(Z * rows, lanes), Z_GROUPS)
    copies = jnp.broadcast_to(got[None], (Y, Z * rows, lanes)).reshape(Y * Z * rows, lanes)
    return spread(copies, Y_GROUPS).reshape(Y, Z * rows, lanes)


def on_device(leaf_blocks, front_entries, child_maps):
    position = lax.axis_index("front")
    cube = lax.axis_index("cube")
    core = cube & 1
    nodes = [jnp.right_shift(cube + 8, h + 1) for h in range(3)]
    sides = [jnp.right_shift(cube, h) & 1 for h in range(3)]
    sc = jnp.stack(
        [n - 1 for n in nodes] + [cube, position, core, jnp.right_shift(cube, 2), cube * 0]
    ).astype(jnp.int32)
    flat = child_maps.reshape(14, KEEP)
    picked = [
        lax.dynamic_index_in_dim(flat, 2 * (n - 1) + s, 0, keepdims=False)
        for n, s in zip(nodes, sides)
    ]
    none = jnp.full((4,), -1, jnp.int32)
    maps = jnp.stack(
        [
            jnp.concatenate([picked[0], none]),
            jnp.concatenate([none, picked[1]]),
            jnp.concatenate([none, picked[2]]),
        ]
    )

    e, ent, ta, tb = call(
        leaf_kernel,
        [SMEM, SMEM, VMEM, VMEM, VMEM],
        [((3, 128, 128), F32), ((3, 128, 128), F32), ((1024, 128), F32), ((1024, 128), F32)],
        [pltpu.VMEM((4, 3840, 128), F32), pltpu.SMEM((128,), jnp.int32)],
        name="leaf",
    )(sc, maps, maps, leaf_blocks, front_entries)

    both = lax.all_gather(e, "cube", axis_index_groups=CORE_GROUPS, axis=0)
    pair = both[0, 1:] + both[1, 1:]
    quad = lax.all_gather(pair, "cube", axis_index_groups=X_GROUPS, axis=0)
    x, sent = call(
        pick_kernel,
        [SMEM] + [VMEM] * 4,
        [((3, 128, 128), F32), ((Z, 24, 128), F32)],
        name="pick",
    )(sc, maps, both, quad, ent)
    g = gather_front(sent, 24)
    g = lax.all_gather(g, "cube", axis_index_groups=CORE_GROUPS, axis=0)

    t_raw = ta + crossed(tb, 1)
    t_raw = t_raw[:512] + crossed(t_raw[512:], 2)
    t_raw = t_raw[:256] + crossed(t_raw[256:], 4)

    f0, v0 = call(
        level0_kernel,
        [SMEM] + [VMEM] * 3,
        [((WIDTH, PAN), F32), ((PAN, 640), BF16)],
        [pltpu.VMEM((PAN, 896), F32), pltpu.VMEM((2, 768, 128), F32)],
        flops=10**9,
        name="level0",
    )(sc, maps, g, x)
    v0s = crossed(v0, 2)
    f1, d1, w1, dh, wh = call(
        level1_kernel,
        [SMEM] + [VMEM] * 5,
        [
            ((WIDTH, PAN), F32),
            ((PAN, 384), F32),
            ((PAN, 256), BF16),
            ((128, 384), F32),
            ((128, 256), BF16),
        ],
        [pltpu.VMEM((PAN, 640), F32), pltpu.VMEM((2, 512, 128), F32)],
        flops=10**9,
        name="level1",
    )(sc, maps, g, x, v0, v0s)
    dh = lax.all_gather(crossed(dh, 4), "cube", axis_index_groups=CORE_GROUPS, axis=0)
    wh = lax.all_gather(crossed(wh, 4), "cube", axis_index_groups=CORE_GROUPS, axis=0)
    f2, thick, vw = call(
        level2_kernel,
        [SMEM] + [VMEM] * 6,
        [((WIDTH, PAN), F32), ((Z, 112, 128), BF16), ((2, 7 * PAN, 128), BF16)],
        [pltpu.VMEM((PAN, 384), F32), pltpu.VMEM((2, 256, 128), F32)],
        flops=10**9,
        name="level2",
    )(sc, g, x, d1, dh, w1, wh)
    thick = gather_front(thick, 112).reshape(Y, Z, 112, 128)
    (piece,) = call(
        top_kernel,
        [VMEM] * 3,
        [((256, 128), F32)],
        [pltpu.VMEM((512, 7 * PAN), F32)],
        name="top",
    )(t_raw, thick, vw)
    pieces = lax.all_gather(piece, "cube", axis=0)
    (top,) = call(last_kernel, [VMEM], [((KEEP, KEEP * N), F32)], name="last")(pieces)
    return jnp.stack([f0, f1, f2])[None], top


def solution(mesh):
    in_specs = (P("cube", "front", None), P(None, "front", None), P())
    out_specs = (P("cube", None, "front", None), P("front", None))
    return jax.shard_map(
        on_device, mesh=mesh, in_specs=in_specs, out_specs=out_specs, check_vma=False
    )
```

```python
import functools

import jax
import jax.numpy as jnp
from jax import lax
from jax.experimental import pallas as pl
from jax.experimental.pallas import tpu as pltpu
from jax.sharding import PartitionSpec as P

F32 = jnp.float32
BF16 = jnp.bfloat16
HIGH = lax.Precision.HIGHEST

N = 64
Z, Y = 16, 4
WIDTH = 64
KEEP = 60
PAN = 256
BLK = 32

Z_GROUPS = [[Y * z + y for z in range(Z)] for y in range(Y)]
Y_GROUPS = [[Y * z + y for y in range(Y)] for z in range(Z)]
CORE_GROUPS = [[0, 1], [2, 3], [4, 5], [6, 7]]
X_GROUPS = [[0, 2, 4, 6], [1, 3, 5, 7]]

VMEM = pl.BlockSpec(memory_space=pltpu.VMEM)
SMEM = pl.BlockSpec(memory_space=pltpu.SMEM)


def iota(shape, dim):
    return lax.broadcasted_iota(jnp.int32, shape, dim)


def split3(x):
    high = x.astype(BF16)
    rest = x - high.astype(F32)
    mid = rest.astype(BF16)
    low = (rest - mid.astype(F32)).astype(BF16)
    return high, mid, low


def dot(a, b, dims):
    return lax.dot_general(a, b, (dims, ((), ())), preferred_element_type=F32)


NN = ((1,), (0,))
NT = ((1,), (1,))
TN = ((0,), (0,))


def onehot_rows(row):
    return (iota((WIDTH, WIDTH), 0) == row).astype(BF16)


def compose(a, b):
    return dot(a, b, NN).astype(BF16)


def tail_table():
    return (iota((WIDTH, WIDTH), 0) + 4 == iota((WIDTH, WIDTH), 1)).astype(BF16)


def unpack(packed):
    full = jnp.concatenate([packed, pltpu.roll(packed, 64, 1)], axis=0)
    return jnp.where(iota(full.shape, 1) < WIDTH, full, 0.0)


def spread_over(x, shape):
    return jnp.broadcast_to(x, shape)


def factor(a_ref, width):
    tile = (8, 128)
    rid = iota(tile, 0)
    count = BLK // 8
    for b in range(PAN // BLK):
        j0 = b * BLK
        lo = j0 // 128 * 128
        wide = width - lo
        tiles = [a_ref[j0 + 8 * t : j0 + 8 * t + 8, lo:width] for t in range(count)]
        for g in range(count):
            c0 = j0 - lo + 8 * g
            cols = [
                [spread_over(tiles[t][:, c0 + k : c0 + k + 1], tile) for t in range(g, count)]
                for k in range(8)
            ]
            for i in range(8):
                inv = 1.0 / spread_over(cols[i][0][i : i + 1, :], tile)
                scale = [c * inv for c in cols[i]]
                scale[0] = jnp.where(rid > i, scale[0], 0.0)
                for k in range(i + 1, 8):
                    s = spread_over(cols[i][0][k : k + 1, :], tile)
                    cols[k] = [c - f * s for c, f in zip(cols[k], scale)]
                row = spread_over(tiles[g][i : i + 1, :], (8, wide))
                for t in range(g, count):
                    f = scale[t - g]
                    tiles[t] = jnp.concatenate(
                        [
                            tiles[t][:, q : q + 128] - f * row[:, q : q + 128]
                            for q in range(0, wide, 128)
                        ],
                        axis=1,
                    )
        rows = jnp.concatenate(tiles, axis=0)
        head = rows[:, 0:128]
        diag = jnp.sum(
            jnp.where(iota(head.shape, 1) == iota(head.shape, 0) + (j0 - lo), head, 0.0),
            axis=1,
            keepdims=True,
        )
        root = lax.rsqrt(diag)
        root = root * (1.5 - 0.5 * diag * root * root)
        rows = rows * root
        a_ref[j0 : j0 + BLK, lo:width] = rows
        r0 = j0 + BLK
        if r0 < PAN:
            nlo = r0 // 128 * 128
            h, m, l = split3(rows[:, nlo - lo :])
            n = PAN - nlo
            left = jnp.concatenate([h, h, m, h, l, m], axis=0)[:, :n]
            right = jnp.concatenate([h, m, h, l, h, m], axis=0)
            done = dot(left, right, TN)
            a_ref[r0:PAN, nlo:width] -= done[r0 - nlo :, :]


def own_columns(own, position):
    p = iota(own.shape, 0)
    t = iota(own.shape, 1)
    kept = jnp.where((t < 4) & (p > t * N + position), 0.0, own)
    return jnp.transpose(kept)[:WIDTH, :]


def rows_of(g_ref, part, first, count, out_ref):
    for r in range(count):
        for y in range(Y):
            for half in range(2):
                out_ref[half, pl.ds(r * N + y, Z, stride=Y), :] = g_ref[y // 2][
                    part, y % 2, pl.ds(half * 12 + first + r, Z, stride=24), :
                ]


def joined(r, first, last):
    return jnp.concatenate([r[0, first:last, :], r[1, first:last, :]], axis=1)


def symmetric(g):
    return jnp.where(iota(g.shape, 1) >= iota(g.shape, 0), jnp.transpose(g), g)


def leaf_kernel(sc, maps_s, maps_v, leaf, entries, e_ref, ent_ref, ta_ref, tb_ref, big, inv):
    cube = sc[3]

    @pl.loop(0, 72)
    def _(k):
        inv[k] = -1

    @pl.loop(0, KEEP)
    def _(v):
        a0 = maps_s[0, v]
        a1 = maps_s[1, a0]
        a2 = maps_s[2, jnp.maximum(a1, 0)]
        code = jnp.where(a0 < 4, a0, jnp.where(a1 < 4, 4 + a1, 8 + a2))
        inv[code] = v

    t0 = onehot_rows(maps_v[0:1, :])
    t1 = compose(onehot_rows(maps_v[1:2, :]), t0)
    t2 = compose(onehot_rows(maps_v[2:3, :]), t1)
    tt = compose(tail_table(), t2)
    table = jnp.concatenate([tt, tt, t0, t0, t1, t1, t2, t2], axis=0).astype(F32)
    table = jnp.transpose(table).astype(BF16)
    table = jnp.concatenate([table, table, table], axis=0)

    pad = jnp.zeros((WIDTH - KEEP, 256), F32)
    for j in range(3840 // 256):
        block = leaf[0, :, j * 256 : (j + 1) * 256]
        block = jnp.concatenate([block, pad], axis=0)
        parts = jnp.concatenate(split3(block), axis=0)
        turned = dot(parts, table, TN)
        for f in range(4):
            big[f, j * 256 : (j + 1) * 256, :] = turned[:, f * 128 : (f + 1) * 128]

    lane = iota((N, 128), 1)
    for h in range(3):
        for k in range(2):
            pieces = []
            for side in range(2):
                v = inv[h * 4 + side * 2 + k]
                got = big[1 + h, pl.ds(jnp.maximum(v, 0), N, stride=KEEP), :]
                pieces.append(jnp.where(v >= 0, got, 0.0))
            e_ref[h, k * N : (k + 1) * N, :] = jnp.where(lane < WIDTH, pieces[0], pieces[1])

    half_lane = iota((N // 2, 128), 1)
    for s in range(8):
        r = jnp.bitwise_xor(s, cube)
        slot = jnp.bitwise_and(r, 2) + jnp.right_shift(r, 2)
        for i in range(8):
            dst = pl.ds(slot * 256 + i, N // 2, stride=8)
            if s * 8 + i < KEEP:
                v = inv[12 + s * 8 + i]
                start = jnp.maximum(v, 0)
                low = big[0, pl.ds(start, N // 2, stride=KEEP), :]
                high = big[0, pl.ds(start + KEEP * N // 2, N // 2, stride=KEEP), :]
                got = jnp.where(v >= 0, jnp.where(half_lane < WIDTH, low, high), 0.0)
            else:
                got = jnp.zeros((N // 2, 128), F32)

            @pl.when(jnp.bitwise_and(r, 1) == 0)
            def _():
                ta_ref[dst, :] = got

            @pl.when(jnp.bitwise_and(r, 1) == 1)
            def _():
                tb_ref[dst, :] = got

    p = iota((PAN, PAN), 0)
    order = (iota((PAN, PAN), 1) == (p % N) * 4 + p // N).astype(BF16)
    for h in range(3):
        e = entries[sc[h]]
        e3 = split3(e)
        placed = dot(order, e3[0], NT) + dot(order, e3[1], NT) + dot(order, e3[2], NT)
        ent_ref[h] = jnp.concatenate([placed[:128], placed[128:]], axis=1)


def pick_kernel(sc, maps_v, e0, e12, ent, x_ref, send_ref):
    core = sc[5]
    pair = sc[6]
    x0 = e0[0, 0] + e0[1, 0] + ent[0]
    q = [e12[x] for x in range(4)]
    low, high = q[0] + q[1], q[2] + q[3]
    x1 = jnp.where(pair == 0, low[0], high[0]) + ent[1]
    x2 = low[1] + high[1] + ent[2]
    x_ref[0], x_ref[1], x_ref[2] = x0, x1, x2
    m1 = onehot_rows(maps_v[1:2, :])
    m2 = onehot_rows(maps_v[2:3, :])
    m21 = compose(m2, m1)
    eye = (iota((WIDTH, WIDTH), 0) == iota((WIDTH, WIDTH), 1)).astype(BF16)

    def first4(tables):
        four = [x.astype(F32)[:8] for x in tables]
        while len(four) < 3:
            four.append(jnp.zeros_like(four[0]))
        return jnp.concatenate(four, axis=0)

    zero = jnp.zeros((8, WIDTH), F32)
    s0 = jnp.where(core == 0, first4([eye, m1, m21]), 0.0)
    s1 = jnp.where(core == 1, first4([eye, m2]), 0.0)
    s2 = jnp.where(
        core == 1, jnp.concatenate([zero, zero, eye.astype(F32)[:8]], axis=0), 0.0
    )
    z = jnp.zeros((24, PAN), F32)
    for s, x in ((s0, x0), (s1, x1), (s2, x2)):
        full = jnp.concatenate([x, pltpu.roll(x, 64, 1)], axis=0)[:, :WIDTH]
        table = s.astype(BF16)
        h, m, l = split3(full)
        z = z + (dot(table, h, NT) + dot(table, m, NT) + dot(table, l, NT))
    rows = jnp.concatenate([z[0:4], z[8:12], z[16:20]], axis=0)
    rows = jnp.concatenate([rows[:, :128], rows[:, 128:]], axis=0)
    for k in range(Z):
        send_ref[k] = rows


def level0_kernel(sc, maps_v, ga, gb, x, f_ref, v_ref, a, r):
    rows_of((ga, gb), 0, 0, 12, r)
    a[:, 0:256] = symmetric(joined(r, 0, 256))
    a[:, 256:768] = jnp.transpose(joined(r, 256, 768))
    a[:, 768:896] = unpack(x[0])
    factor(a, 896)
    own = a[:, 768:896]
    f_ref[...] = own_columns(own, sc[4])
    m1 = onehot_rows(maps_v[1:2, :])
    v_ref[:, 0:512] = a[:, 256:768].astype(BF16)
    moved = dot(own[:, :WIDTH].astype(BF16), m1, NT)
    v_ref[:, 512:640] = jnp.concatenate([moved, jnp.zeros_like(moved)], axis=1).astype(BF16)


def level1_kernel(sc, maps_v, ga, gb, x, v0, v0s, f_ref, d_ref, half_ref, a, r):
    rows_of((ga, gb), 1, 0, 8, r)
    a[:, 0:256] = symmetric(joined(r, 0, 256))
    a[:, 256:512] = jnp.transpose(joined(r, 256, 512))
    a[:, 512:640] = unpack(x[1])
    mine, other = v0[...], v0s[...]
    a[...] -= dot(mine[:, 0:256], mine, TN) + dot(other[:, 0:256], other, TN)
    factor(a, 640)
    own = a[:, 512:640]
    f_ref[...] = own_columns(own, sc[4])
    m2 = onehot_rows(maps_v[2:3, :])
    moved = [
        dot(mine[:, 512 : 512 + WIDTH], m2, NT).astype(BF16),
        dot(other[:, 512 : 512 + WIDTH], m2, NT).astype(BF16),
        dot(own[:, :WIDTH].astype(BF16), m2, NT).astype(BF16),
    ]
    cols = [mine[:, 256:512], other[:, 256:512], a[:, 256:512].astype(BF16)]
    zero = jnp.zeros((PAN, WIDTH), F32)
    right0 = [jnp.concatenate([c.astype(F32), m.astype(F32), zero], axis=1) for c, m in zip(cols, moved)]
    total = jnp.zeros((PAN, 384), F32)
    for c, right in zip(cols, right0):
        total = total + dot(c, right.astype(BF16), TN)
    d_ref[:, 0:256] = total[:, 0:256]
    d_ref[:, 256:384] = jnp.concatenate(
        [total[:, 256 : 256 + WIDTH], moved[0].astype(F32)], axis=1
    )
    d_ref[:, 384:512] = jnp.concatenate(
        [moved[1].astype(F32), moved[2].astype(F32)], axis=1
    )
    first = pl.multiple_of(sc[5] * 128, 128)
    half_ref[...] = d_ref[pl.ds(first, 128), :]


def level2_kernel(sc, ga, gb, x, d, ds, f0, f1, f_ref, send_ref, vw_ref, a, r):
    rows_of((ga, gb), 1, 8, 4, r)
    sib = jnp.concatenate([ds[0], ds[1]], axis=0)
    mine = d[...]
    sub = mine[:, 0:384] + sib[:, 0:384]
    a[:, 0:256] = symmetric(joined(r, 0, 256)) - sub[:, 0:256]
    a[:, 256:384] = jnp.where(
        iota((PAN, 128), 1) < WIDTH, unpack(x[2]) - sub[:, 256:384], 0.0
    )
    factor(a, 384)
    own = a[:, 256:384]
    f_ref[0] = f0[...]
    f_ref[1] = f1[...]
    f_ref[2] = own_columns(own, sc[4])
    pieces = [
        m[:, first : first + WIDTH].astype(BF16)
        for m in (mine, sib)
        for first in (320, 384, 448)
    ]
    pieces.append(own[:, :WIDTH].astype(BF16))
    first = 4 + 8 * sc[3]
    pick = (iota((8, WIDTH), 0) + first == iota((8, WIDTH), 1)).astype(BF16)
    thick = jnp.concatenate([dot(pick, v, NT) for v in pieces], axis=0)
    thick = jnp.concatenate([thick[:, :128], thick[:, 128:]], axis=0).astype(BF16)
    send_ref[...] = thick
    src = iota((WIDTH, 128), 0)
    dst = iota((WIDTH, 128), 1)
    low = (src == dst + 4).astype(BF16)
    low = jnp.where(dst < KEEP, low, jnp.zeros_like(low))
    high = ((src == dst - 60) & (dst >= WIDTH)).astype(BF16)
    for n, v in enumerate(pieces):
        vw_ref[0, n * PAN : (n + 1) * PAN, :] = dot(v, low, NN).astype(BF16)
        vw_ref[1, n * PAN : (n + 1) * PAN, :] = dot(v, high, NN).astype(BF16)


def top_kernel(t_raw, got, vw, out, big):
    for y in range(Y):
        for z in range(Z):
            block = got[y, z].astype(F32)
            d = z * Y + y
            for n in range(7):
                for half in range(2):
                    first = half * 56 + n * 8
                    big[d * 8 : d * 8 + 8, (n * 2 + half) * 128 : (n * 2 + half + 1) * 128] = (
                        block[first : first + 8, :]
                    )
    low = dot(big[0:256, :].astype(BF16), vw[0], NN)
    high = dot(big[256:512, :].astype(BF16), vw[1], NN)
    piece = t_raw[...] - (low + high)
    last = piece[248:256, :]
    lane = iota((8, 128), 1)
    for t in range(31):
        rows = piece[8 * t : 8 * t + 8, :]
        if t < 16:
            one = pltpu.roll(last, (60 - 8 * t) % 128, 1)
            two = pltpu.roll(last, (120 - 8 * t) % 128, 1)
            rows = jnp.where(
                lane >= 124, two, jnp.where((lane >= 60) & (lane < 64), one, rows)
            )
        out[8 * t : 8 * t + 8, :] = rows


def last_kernel(t, out):
    lane = iota((8, 128), 1)
    ends = []
    for s in range(8):
        end = jnp.zeros((8, 128), F32)
        for k in range(16):
            rows = t[s, 8 * k : 8 * k + 8, :]
            one = pltpu.roll(rows, (8 * k - 60) % 128, 1)
            two = pltpu.roll(rows, (8 * k - 120) % 128, 1)
            end = jnp.where(lane // 4 == 2 * k, one, jnp.where(lane // 4 == 2 * k + 1, two, end))
        ends.append(end)
    for d in range(N // 2):
        if d < N // 2 - 1:
            block = jnp.concatenate([t[s, d * 8 : d * 8 + 8, :] for s in range(8)], axis=0)
        else:
            block = jnp.concatenate(ends, axis=0)
        turned = jnp.transpose(block)
        out[:, d * KEEP : (d + 1) * KEEP] = turned[0:KEEP, 0:KEEP]
        d2 = d + N // 2
        out[:, d2 * KEEP : (d2 + 1) * KEEP] = turned[WIDTH : WIDTH + KEEP, 0:KEEP]


def call(kernel, specs, outs, scratch=(), flops=10**8, name=None):
    return pl.pallas_call(
        kernel,
        in_specs=specs,
        out_specs=[VMEM] * len(outs),
        out_shape=[jax.ShapeDtypeStruct(s, t) for s, t in outs],
        scratch_shapes=list(scratch),
        compiler_params=pltpu.CompilerParams(vmem_limit_bytes=48 * 2**20),
        cost_estimate=pl.CostEstimate(flops=flops, bytes_accessed=4 * 10**6, transcendentals=0),
        name=name,
    )


def crossed(value, mask):
    return lax.ppermute(value, "cube", [(c, c ^ mask) for c in range(8)])


def spread(value, axis_groups):
    return lax.all_to_all(value, "front", 0, 0, axis_index_groups=axis_groups, tiled=True)


def gather_front(sent, rows):
    lanes = sent.shape[-1]
    got = spread(sent.reshape(Z * rows, lanes), Z_GROUPS)
    copies = jnp.broadcast_to(got[None], (Y, Z * rows, lanes)).reshape(Y * Z * rows, lanes)
    return spread(copies, Y_GROUPS).reshape(Y, Z * rows, lanes)


def on_device(leaf_blocks, front_entries, child_maps):
    position = lax.axis_index("front")
    cube = lax.axis_index("cube")
    core = cube & 1
    nodes = [jnp.right_shift(cube + 8, h + 1) for h in range(3)]
    sides = [jnp.right_shift(cube, h) & 1 for h in range(3)]
    sc = jnp.stack(
        [n - 1 for n in nodes] + [cube, position, core, jnp.right_shift(cube, 2), cube * 0]
    ).astype(jnp.int32)
    flat = child_maps.reshape(14, KEEP)
    picked = [
        lax.dynamic_index_in_dim(flat, 2 * (n - 1) + s, 0, keepdims=False)
        for n, s in zip(nodes, sides)
    ]
    none = jnp.full((4,), -1, jnp.int32)
    maps = jnp.stack(
        [
            jnp.concatenate([picked[0], none]),
            jnp.concatenate([none, picked[1]]),
            jnp.concatenate([none, picked[2]]),
        ]
    )

    e, ent, ta, tb = call(
        leaf_kernel,
        [SMEM, SMEM, VMEM, VMEM, VMEM],
        [((3, 128, 128), F32), ((3, 128, 128), F32), ((1024, 128), F32), ((1024, 128), F32)],
        [pltpu.VMEM((4, 3840, 128), F32), pltpu.SMEM((128,), jnp.int32)],
        name="leaf",
    )(sc, maps, maps, leaf_blocks, front_entries)

    both = lax.all_gather(e, "cube", axis_index_groups=CORE_GROUPS, axis=0)
    pair = both[0, 1:] + both[1, 1:]
    quad = lax.all_gather(pair, "cube", axis_index_groups=X_GROUPS, axis=0)
    x, sent = call(
        pick_kernel,
        [SMEM] + [VMEM] * 4,
        [((3, 128, 128), F32), ((Z, 24, 128), F32)],
        name="pick",
    )(sc, maps, both, quad, ent)
    g = gather_front(sent, 24)
    ga, gb = [
        lax.all_gather(part, "cube", axis_index_groups=CORE_GROUPS, axis=0)
        for part in (g[:2], g[2:])
    ]

    t_raw = ta + crossed(tb, 1)
    t_raw = t_raw[:512] + crossed(t_raw[512:], 2)
    t_raw = t_raw[:256] + crossed(t_raw[256:], 4)

    f0, v0 = call(
        level0_kernel,
        [SMEM] + [VMEM] * 4,
        [((WIDTH, PAN), F32), ((PAN, 640), BF16)],
        [pltpu.VMEM((PAN, 896), F32), pltpu.VMEM((2, 768, 128), F32)],
        flops=10**9,
        name="level0",
    )(sc, maps, ga, gb, x)
    v0s = crossed(v0, 2)
    f1, d1, half = call(
        level1_kernel,
        [SMEM] + [VMEM] * 6,
        [((WIDTH, PAN), F32), ((PAN, 512), F32), ((128, 512), F32)],
        [pltpu.VMEM((PAN, 640), F32), pltpu.VMEM((2, 512, 128), F32)],
        flops=10**9,
        name="level1",
    )(sc, maps, ga, gb, x, v0, v0s)
    d1s = lax.all_gather(crossed(half, 4), "cube", axis_index_groups=CORE_GROUPS, axis=0)
    factors, thick, vw = call(
        level2_kernel,
        [SMEM] + [VMEM] * 7,
        [((3, WIDTH, PAN), F32), ((112, 128), BF16), ((2, 7 * PAN, 128), BF16)],
        [pltpu.VMEM((PAN, 384), F32), pltpu.VMEM((2, 256, 128), F32)],
        flops=10**9,
        name="level2",
    )(sc, ga, gb, x, d1, d1s, f0, f1)
    thick = lax.all_gather(thick, "front", axis_index_groups=Z_GROUPS, axis=0, tiled=True)
    copies = jnp.broadcast_to(thick[None], (Y, Z * 112, 128)).reshape(Y * Z * 112, 128)
    thick = spread(copies, Y_GROUPS).reshape(Y, Z, 112, 128)
    (piece,) = call(
        top_kernel,
        [VMEM] * 3,
        [((248, 128), F32)],
        [pltpu.VMEM((512, 7 * PAN), F32)],
        name="top",
    )(t_raw, thick, vw)
    pieces = lax.all_gather(piece, "cube", axis=0)
    (top,) = call(last_kernel, [VMEM], [((KEEP, KEEP * N), F32)], name="last")(pieces)
    return factors[None], top


def solution(mesh):
    in_specs = (P("cube", "front", None), P(None, "front", None), P())
    out_specs = (P("cube", None, "front", None), P("front", None))
    return jax.shard_map(
        on_device, mesh=mesh, in_specs=in_specs, out_specs=out_specs, check_vma=False
    )
```

```python
import functools

import jax
import jax.numpy as jnp
from jax import lax
from jax.experimental import pallas as pl
from jax.experimental.pallas import tpu as pltpu
from jax.sharding import PartitionSpec as P

F32 = jnp.float32
BF16 = jnp.bfloat16
HIGH = lax.Precision.HIGHEST

N = 64
FAR, NEAR = 8, 8
WIDTH = 64
KEEP = 60
PAN = 256
BLK = 32

FAR_GROUPS = [[NEAR * far + near for far in range(FAR)] for near in range(NEAR)]
NEAR_GROUPS = [[NEAR * far + near for near in range(NEAR)] for far in range(FAR)]
CORE_GROUPS = [[0, 1], [2, 3], [4, 5], [6, 7]]
X_GROUPS = [[0, 2, 4, 6], [1, 3, 5, 7]]

VMEM = pl.BlockSpec(memory_space=pltpu.VMEM)
SMEM = pl.BlockSpec(memory_space=pltpu.SMEM)


def iota(shape, dim):
    return lax.broadcasted_iota(jnp.int32, shape, dim)


def split3(x):
    high = x.astype(BF16)
    rest = x - high.astype(F32)
    mid = rest.astype(BF16)
    low = (rest - mid.astype(F32)).astype(BF16)
    return high, mid, low


def dot(a, b, dims):
    return lax.dot_general(a, b, (dims, ((), ())), preferred_element_type=F32)


NN = ((1,), (0,))
NT = ((1,), (1,))
TN = ((0,), (0,))


def onehot_rows(row):
    return (iota((WIDTH, WIDTH), 0) == row).astype(BF16)


def compose(a, b):
    return dot(a, b, NN).astype(BF16)


def tail_table():
    return (iota((WIDTH, WIDTH), 0) + 4 == iota((WIDTH, WIDTH), 1)).astype(BF16)


def unpack(packed):
    full = jnp.concatenate([packed, pltpu.roll(packed, 64, 1)], axis=0)
    return jnp.where(iota(full.shape, 1) < WIDTH, full, 0.0)


def spread_over(x, shape):
    return jnp.broadcast_to(x, shape)


def factor(a_ref, width):
    tile = (8, 128)
    rid = iota(tile, 0)
    count = BLK // 8
    for b in range(PAN // BLK):
        j0 = b * BLK
        lo = j0 // 128 * 128
        wide = width - lo
        tiles = [a_ref[j0 + 8 * t : j0 + 8 * t + 8, lo:width] for t in range(count)]
        for g in range(count):
            c0 = j0 - lo + 8 * g
            cols = [
                [spread_over(tiles[t][:, c0 + k : c0 + k + 1], tile) for t in range(g, count)]
                for k in range(8)
            ]
            for i in range(8):
                inv = 1.0 / spread_over(cols[i][0][i : i + 1, :], tile)
                scale = [c * inv for c in cols[i]]
                scale[0] = jnp.where(rid > i, scale[0], 0.0)
                for k in range(i + 1, 8):
                    s = spread_over(cols[i][0][k : k + 1, :], tile)
                    cols[k] = [c - f * s for c, f in zip(cols[k], scale)]
                row = spread_over(tiles[g][i : i + 1, :], (8, wide))
                for t in range(g, count):
                    f = scale[t - g]
                    tiles[t] = jnp.concatenate(
                        [
                            tiles[t][:, q : q + 128] - f * row[:, q : q + 128]
                            for q in range(0, wide, 128)
                        ],
                        axis=1,
                    )
        rows = jnp.concatenate(tiles, axis=0)
        head = rows[:, 0:128]
        diag = jnp.sum(
            jnp.where(iota(head.shape, 1) == iota(head.shape, 0) + (j0 - lo), head, 0.0),
            axis=1,
            keepdims=True,
        )
        root = lax.rsqrt(diag)
        root = root * (1.5 - 0.5 * diag * root * root)
        rows = rows * root
        a_ref[j0 : j0 + BLK, lo:width] = rows
        r0 = j0 + BLK
        if r0 < PAN:
            nlo = r0 // 128 * 128
            h, m, l = split3(rows[:, nlo - lo :])
            n = PAN - nlo
            left = jnp.concatenate([h, h, m, h, l, m], axis=0)[:, :n]
            right = jnp.concatenate([h, m, h, l, h, m], axis=0)
            done = dot(left, right, TN)
            a_ref[r0:PAN, nlo:width] -= done[r0 - nlo :, :]


def own_columns(own, position):
    p = iota(own.shape, 0)
    t = iota(own.shape, 1)
    kept = jnp.where((t < 4) & (p > t * N + position), 0.0, own)
    return jnp.transpose(kept)[:WIDTH, :]


def rows_of(g_ref, part, first, count, out_ref):
    for r in range(count):
        for near in range(NEAR):
            for half in range(2):
                out_ref[half, pl.ds(r * N + near, FAR, stride=NEAR), :] = g_ref[near // 4][
                    part, near % 4, pl.ds(half * 12 + first + r, FAR, stride=24), :
                ]


def joined(r, first, last):
    return jnp.concatenate([r[0, first:last, :], r[1, first:last, :]], axis=1)


def symmetric(g):
    return jnp.where(iota(g.shape, 1) >= iota(g.shape, 0), jnp.transpose(g), g)


def leaf_kernel(sc, maps_s, maps_v, leaf, entries, e_ref, ent_ref, ta_ref, tb_ref, big, inv):
    cube = sc[3]

    @pl.loop(0, 72)
    def _(k):
        inv[k] = -1

    @pl.loop(0, KEEP)
    def _(v):
        a0 = maps_s[0, v]
        a1 = maps_s[1, a0]
        a2 = maps_s[2, jnp.maximum(a1, 0)]
        code = jnp.where(a0 < 4, a0, jnp.where(a1 < 4, 4 + a1, 8 + a2))
        inv[code] = v

    t0 = onehot_rows(maps_v[0:1, :])
    t1 = compose(onehot_rows(maps_v[1:2, :]), t0)
    t2 = compose(onehot_rows(maps_v[2:3, :]), t1)
    tt = compose(tail_table(), t2)
    table = jnp.concatenate([tt, tt, t0, t0, t1, t1, t2, t2], axis=0).astype(F32)
    table = jnp.transpose(table).astype(BF16)
    table = jnp.concatenate([table, table, table], axis=0)

    pad = jnp.zeros((WIDTH - KEEP, 256), F32)
    for j in range(3840 // 256):
        block = leaf[0, :, j * 256 : (j + 1) * 256]
        block = jnp.concatenate([block, pad], axis=0)
        parts = jnp.concatenate(split3(block), axis=0)
        turned = dot(parts, table, TN)
        for f in range(4):
            big[f, j * 256 : (j + 1) * 256, :] = turned[:, f * 128 : (f + 1) * 128]

    lane = iota((N, 128), 1)
    for h in range(3):
        for k in range(2):
            pieces = []
            for side in range(2):
                v = inv[h * 4 + side * 2 + k]
                got = big[1 + h, pl.ds(jnp.maximum(v, 0), N, stride=KEEP), :]
                pieces.append(jnp.where(v >= 0, got, 0.0))
            e_ref[h, k * N : (k + 1) * N, :] = jnp.where(lane < WIDTH, pieces[0], pieces[1])

    half_lane = iota((N // 2, 128), 1)
    for s in range(8):
        r = jnp.bitwise_xor(s, cube)
        slot = jnp.bitwise_and(r, 2) + jnp.right_shift(r, 2)
        for i in range(8):
            dst = pl.ds(slot * 256 + i, N // 2, stride=8)
            if s * 8 + i < KEEP:
                v = inv[12 + s * 8 + i]
                start = jnp.maximum(v, 0)
                low = big[0, pl.ds(start, N // 2, stride=KEEP), :]
                high = big[0, pl.ds(start + KEEP * N // 2, N // 2, stride=KEEP), :]
                got = jnp.where(v >= 0, jnp.where(half_lane < WIDTH, low, high), 0.0)
            else:
                got = jnp.zeros((N // 2, 128), F32)

            @pl.when(jnp.bitwise_and(r, 1) == 0)
            def _():
                ta_ref[dst, :] = got

            @pl.when(jnp.bitwise_and(r, 1) == 1)
            def _():
                tb_ref[dst, :] = got

    p = iota((PAN, PAN), 0)
    order = (iota((PAN, PAN), 1) == (p % N) * 4 + p // N).astype(BF16)
    for h in range(3):
        e = entries[sc[h]]
        e3 = split3(e)
        placed = dot(order, e3[0], NT) + dot(order, e3[1], NT) + dot(order, e3[2], NT)
        ent_ref[h] = jnp.concatenate([placed[:128], placed[128:]], axis=1)


def pick_kernel(sc, maps_v, e0, e12, ent, x_ref, send_ref):
    core = sc[5]
    pair = sc[6]
    x0 = e0[0, 0] + e0[1, 0] + ent[0]
    q = [e12[x] for x in range(4)]
    low, high = q[0] + q[1], q[2] + q[3]
    x1 = jnp.where(pair == 0, low[0], high[0]) + ent[1]
    x2 = low[1] + high[1] + ent[2]
    x_ref[0], x_ref[1], x_ref[2] = x0, x1, x2
    m1 = onehot_rows(maps_v[1:2, :])
    m2 = onehot_rows(maps_v[2:3, :])
    m21 = compose(m2, m1)
    eye = (iota((WIDTH, WIDTH), 0) == iota((WIDTH, WIDTH), 1)).astype(BF16)

    def first4(tables):
        four = [x.astype(F32)[:8] for x in tables]
        while len(four) < 3:
            four.append(jnp.zeros_like(four[0]))
        return jnp.concatenate(four, axis=0)

    zero = jnp.zeros((8, WIDTH), F32)
    s0 = jnp.where(core == 0, first4([eye, m1, m21]), 0.0)
    s1 = jnp.where(core == 1, first4([eye, m2]), 0.0)
    s2 = jnp.where(
        core == 1, jnp.concatenate([zero, zero, eye.astype(F32)[:8]], axis=0), 0.0
    )
    z = jnp.zeros((24, PAN), F32)
    for s, x in ((s0, x0), (s1, x1), (s2, x2)):
        full = jnp.concatenate([x, pltpu.roll(x, 64, 1)], axis=0)[:, :WIDTH]
        table = s.astype(BF16)
        h, m, l = split3(full)
        z = z + (dot(table, h, NT) + dot(table, m, NT) + dot(table, l, NT))
    rows = jnp.concatenate([z[0:4], z[8:12], z[16:20]], axis=0)
    rows = jnp.concatenate([rows[:, :128], rows[:, 128:]], axis=0)
    for k in range(FAR):
        send_ref[k] = rows


def level0_kernel(sc, maps_v, ga, gb, x, ta, tr, f_ref, v_ref, tk_ref, ts_ref, a, r):
    tk_ref[...] = ta[0:512, :] + tr[0:512, :]
    ts_ref[...] = ta[512:1024, :] + tr[512:1024, :]
    rows_of((ga, gb), 0, 0, 12, r)
    a[:, 0:256] = symmetric(joined(r, 0, 256))
    a[:, 256:768] = jnp.transpose(joined(r, 256, 768))
    a[:, 768:896] = unpack(x[0])
    factor(a, 896)
    own = a[:, 768:896]
    f_ref[...] = own_columns(own, sc[4])
    m1 = onehot_rows(maps_v[1:2, :])
    v_ref[:, 0:512] = a[:, 256:768].astype(BF16)
    moved = dot(own[:, :WIDTH].astype(BF16), m1, NT)
    v_ref[:, 512:640] = jnp.concatenate([moved, jnp.zeros_like(moved)], axis=1).astype(BF16)


def level1_kernel(sc, maps_v, ga, gb, x, v0, v0s, f_ref, d_ref, half_ref, a, r):
    rows_of((ga, gb), 1, 0, 8, r)
    a[:, 0:256] = symmetric(joined(r, 0, 256))
    a[:, 256:512] = jnp.transpose(joined(r, 256, 512))
    a[:, 512:640] = unpack(x[1])
    mine, other = v0[...], v0s[...]
    a[...] -= dot(mine[:, 0:256], mine, TN) + dot(other[:, 0:256], other, TN)
    factor(a, 640)
    own = a[:, 512:640]
    f_ref[...] = own_columns(own, sc[4])
    m2 = onehot_rows(maps_v[2:3, :])
    moved = [
        dot(mine[:, 512 : 512 + WIDTH], m2, NT).astype(BF16),
        dot(other[:, 512 : 512 + WIDTH], m2, NT).astype(BF16),
        dot(own[:, :WIDTH].astype(BF16), m2, NT).astype(BF16),
    ]
    cols = [mine[:, 256:512], other[:, 256:512], a[:, 256:512].astype(BF16)]
    zero = jnp.zeros((PAN, WIDTH), F32)
    right0 = [jnp.concatenate([c.astype(F32), m.astype(F32), zero], axis=1) for c, m in zip(cols, moved)]
    total = jnp.zeros((PAN, 384), F32)
    for c, right in zip(cols, right0):
        total = total + dot(c, right.astype(BF16), TN)
    d_ref[:, 0:256] = total[:, 0:256]
    d_ref[:, 256:384] = jnp.concatenate(
        [total[:, 256 : 256 + WIDTH], moved[0].astype(F32)], axis=1
    )
    d_ref[:, 384:512] = jnp.concatenate(
        [moved[1].astype(F32), moved[2].astype(F32)], axis=1
    )
    first = pl.multiple_of(sc[5] * 128, 128)
    half_ref[...] = d_ref[pl.ds(first, 128), :]


def level2_kernel(
    sc, ga, gb, x, d, ds, f0, f1, tk, tr, f_ref, send_ref, vw_ref, tk_ref, ts_ref, a, r
):
    tk_ref[...] = tk[0:256, :] + tr[0:256, :]
    ts_ref[...] = tk[256:512, :] + tr[256:512, :]
    rows_of((ga, gb), 1, 8, 4, r)
    sib = jnp.concatenate([ds[0], ds[1]], axis=0)
    mine = d[...]
    sub = mine[:, 0:384] + sib[:, 0:384]
    a[:, 0:256] = symmetric(joined(r, 0, 256)) - sub[:, 0:256]
    a[:, 256:384] = jnp.where(
        iota((PAN, 128), 1) < WIDTH, unpack(x[2]) - sub[:, 256:384], 0.0
    )
    factor(a, 384)
    own = a[:, 256:384]
    f_ref[0] = f0[...]
    f_ref[1] = f1[...]
    f_ref[2] = own_columns(own, sc[4])
    pieces = [
        m[:, first : first + WIDTH].astype(BF16)
        for m in (mine, sib)
        for first in (320, 384, 448)
    ]
    pieces.append(own[:, :WIDTH].astype(BF16))
    first = 4 + 8 * sc[3]
    pick = (iota((8, WIDTH), 0) + first == iota((8, WIDTH), 1)).astype(BF16)
    thick = jnp.concatenate([dot(pick, v, NT) for v in pieces], axis=0)
    thick = jnp.concatenate([thick[:, :128], thick[:, 128:]], axis=0).astype(BF16)
    for k in range(FAR):
        send_ref[k] = thick
    src = iota((WIDTH, 128), 0)
    dst = iota((WIDTH, 128), 1)
    low = (src == dst + 4).astype(BF16)
    low = jnp.where(dst < KEEP, low, jnp.zeros_like(low))
    high = ((src == dst - 60) & (dst >= WIDTH)).astype(BF16)
    for n, v in enumerate(pieces):
        vw_ref[0, n * PAN : (n + 1) * PAN, :] = dot(v, low, NN).astype(BF16)
        vw_ref[1, n * PAN : (n + 1) * PAN, :] = dot(v, high, NN).astype(BF16)


def top_kernel(tk, tr, got, vw, out, big):
    for near in range(NEAR):
        for far in range(FAR):
            block = got[near, far].astype(F32)
            d = far * NEAR + near
            for n in range(7):
                for half in range(2):
                    first = half * 56 + n * 8
                    big[d * 8 : d * 8 + 8, (n * 2 + half) * 128 : (n * 2 + half + 1) * 128] = (
                        block[first : first + 8, :]
                    )
    low = dot(big[0:256, :].astype(BF16), vw[0], NN)
    high = dot(big[256:512, :].astype(BF16), vw[1], NN)
    piece = tk[...] + tr[...] - (low + high)
    last = piece[248:256, :]
    lane = iota((8, 128), 1)
    for t in range(31):
        rows = piece[8 * t : 8 * t + 8, :]
        if t < 16:
            one = pltpu.roll(last, (60 - 8 * t) % 128, 1)
            two = pltpu.roll(last, (120 - 8 * t) % 128, 1)
            rows = jnp.where(
                lane >= 124, two, jnp.where((lane >= 60) & (lane < 64), one, rows)
            )
        out[8 * t : 8 * t + 8, :] = rows


def last_kernel(t, out):
    lane = iota((8, 128), 1)
    ends = []
    for s in range(8):
        end = jnp.zeros((8, 128), F32)
        for k in range(16):
            rows = t[s, 8 * k : 8 * k + 8, :]
            one = pltpu.roll(rows, (8 * k - 60) % 128, 1)
            two = pltpu.roll(rows, (8 * k - 120) % 128, 1)
            end = jnp.where(lane // 4 == 2 * k, one, jnp.where(lane // 4 == 2 * k + 1, two, end))
        ends.append(end)
    for d in range(N // 2):
        if d < N // 2 - 1:
            block = jnp.concatenate([t[s, d * 8 : d * 8 + 8, :] for s in range(8)], axis=0)
        else:
            block = jnp.concatenate(ends, axis=0)
        turned = jnp.transpose(block)
        out[:, d * KEEP : (d + 1) * KEEP] = turned[0:KEEP, 0:KEEP]
        d2 = d + N // 2
        out[:, d2 * KEEP : (d2 + 1) * KEEP] = turned[WIDTH : WIDTH + KEEP, 0:KEEP]


def call(kernel, specs, outs, scratch=(), flops=10**8, name=None):
    return pl.pallas_call(
        kernel,
        in_specs=specs,
        out_specs=[VMEM] * len(outs),
        out_shape=[jax.ShapeDtypeStruct(s, t) for s, t in outs],
        scratch_shapes=list(scratch),
        compiler_params=pltpu.CompilerParams(vmem_limit_bytes=48 * 2**20),
        cost_estimate=pl.CostEstimate(flops=flops, bytes_accessed=4 * 10**6, transcendentals=0),
        name=name,
    )


def crossed(value, mask):
    return lax.ppermute(value, "cube", [(c, c ^ mask) for c in range(8)])


def spread(value, axis_groups):
    return lax.all_to_all(value, "front", 0, 0, axis_index_groups=axis_groups, tiled=True)


def gather_front(sent, rows):
    lanes = sent.shape[-1]
    got = spread(sent.reshape(FAR * rows, lanes), FAR_GROUPS)
    copies = jnp.broadcast_to(got[None], (NEAR, FAR * rows, lanes))
    got = spread(copies.reshape(NEAR * FAR * rows, lanes), NEAR_GROUPS)
    return got.reshape(NEAR, FAR * rows, lanes)


def on_device(leaf_blocks, front_entries, child_maps):
    position = lax.axis_index("front")
    cube = lax.axis_index("cube")
    core = cube & 1
    nodes = [jnp.right_shift(cube + 8, h + 1) for h in range(3)]
    sides = [jnp.right_shift(cube, h) & 1 for h in range(3)]
    sc = jnp.stack(
        [n - 1 for n in nodes] + [cube, position, core, jnp.right_shift(cube, 2), cube * 0]
    ).astype(jnp.int32)
    flat = child_maps.reshape(14, KEEP)
    picked = [
        lax.dynamic_index_in_dim(flat, 2 * (n - 1) + s, 0, keepdims=False)
        for n, s in zip(nodes, sides)
    ]
    none = jnp.full((4,), -1, jnp.int32)
    maps = jnp.stack(
        [
            jnp.concatenate([picked[0], none]),
            jnp.concatenate([none, picked[1]]),
            jnp.concatenate([none, picked[2]]),
        ]
    )

    e, ent, ta, tb = call(
        leaf_kernel,
        [SMEM, SMEM, VMEM, VMEM, VMEM],
        [((3, 128, 128), F32), ((3, 128, 128), F32), ((1024, 128), F32), ((1024, 128), F32)],
        [pltpu.VMEM((4, 3840, 128), F32), pltpu.SMEM((128,), jnp.int32)],
        name="leaf",
    )(sc, maps, maps, leaf_blocks, front_entries)

    both = lax.all_gather(e, "cube", axis_index_groups=CORE_GROUPS, axis=0)
    pair = both[0, 1:] + both[1, 1:]
    quad = lax.all_gather(pair, "cube", axis_index_groups=X_GROUPS, axis=0)
    x, sent = call(
        pick_kernel,
        [SMEM] + [VMEM] * 4,
        [((3, 128, 128), F32), ((FAR, 24, 128), F32)],
        name="pick",
    )(sc, maps, both, quad, ent)
    g = gather_front(sent, 24)
    ga, gb = [
        lax.all_gather(part, "cube", axis_index_groups=CORE_GROUPS, axis=0)
        for part in (g[:4], g[4:])
    ]

    tr = crossed(tb, 1)
    f0, v0, tk, ts = call(
        level0_kernel,
        [SMEM] + [VMEM] * 6,
        [((WIDTH, PAN), F32), ((PAN, 640), BF16), ((512, 128), F32), ((512, 128), F32)],
        [pltpu.VMEM((PAN, 896), F32), pltpu.VMEM((2, 768, 128), F32)],
        flops=10**9,
        name="level0",
    )(sc, maps, ga, gb, x, ta, tr)
    v0s, ts = lax.optimization_barrier((crossed(v0, 2), ts))
    tr = crossed(ts, 2)
    f1, d1, half = call(
        level1_kernel,
        [SMEM] + [VMEM] * 6,
        [((WIDTH, PAN), F32), ((PAN, 512), F32), ((128, 512), F32)],
        [pltpu.VMEM((PAN, 640), F32), pltpu.VMEM((2, 512, 128), F32)],
        flops=10**9,
        name="level1",
    )(sc, maps, ga, gb, x, v0, v0s)
    half, tr = lax.optimization_barrier((half, tr))
    d1s = lax.all_gather(crossed(half, 4), "cube", axis_index_groups=CORE_GROUPS, axis=0)
    factors, thick, vw, tk, ts = call(
        level2_kernel,
        [SMEM] + [VMEM] * 9,
        [
            ((3, WIDTH, PAN), F32),
            ((FAR, 112, 128), BF16),
            ((2, 7 * PAN, 128), BF16),
            ((256, 128), F32),
            ((256, 128), F32),
        ],
        [pltpu.VMEM((PAN, 384), F32), pltpu.VMEM((2, 256, 128), F32)],
        flops=10**9,
        name="level2",
    )(sc, ga, gb, x, d1, d1s, f0, f1, tk, tr)
    tr = crossed(ts, 4)
    thick = gather_front(thick, 112).reshape(NEAR, FAR, 112, 128)
    (piece,) = call(
        top_kernel,
        [VMEM] * 4,
        [((248, 128), F32)],
        [pltpu.VMEM((512, 7 * PAN), F32)],
        name="top",
    )(tk, tr, thick, vw)
    pieces = lax.all_gather(piece, "cube", axis=0)
    (top,) = call(last_kernel, [VMEM], [((KEEP, KEEP * N), F32)], name="last")(pieces)
    return factors[None], top


def solution(mesh):
    in_specs = (P("cube", "front", None), P(None, "front", None), P())
    out_specs = (P("cube", None, "front", None), P("front", None))
    return jax.shard_map(
        on_device, mesh=mesh, in_specs=in_specs, out_specs=out_specs, check_vma=False
    )
```

```python
import functools

import jax
import jax.numpy as jnp
from jax import lax
from jax.experimental import pallas as pl
from jax.experimental.pallas import tpu as pltpu
from jax.sharding import PartitionSpec as P

F32 = jnp.float32
BF16 = jnp.bfloat16
HIGH = lax.Precision.HIGHEST

N = 64
FAR, NEAR = 8, 8
WIDTH = 64
KEEP = 60
PAN = 256
BLK = 32

FAR_GROUPS = [[NEAR * far + near for far in range(FAR)] for near in range(NEAR)]
NEAR_GROUPS = [[NEAR * far + near for near in range(NEAR)] for far in range(FAR)]
CORE_GROUPS = [[0, 1], [2, 3], [4, 5], [6, 7]]

VMEM = pl.BlockSpec(memory_space=pltpu.VMEM)
SMEM = pl.BlockSpec(memory_space=pltpu.SMEM)


def iota(shape, dim):
    return lax.broadcasted_iota(jnp.int32, shape, dim)


def split3(x):
    high = x.astype(BF16)
    rest = x - high.astype(F32)
    mid = rest.astype(BF16)
    low = (rest - mid.astype(F32)).astype(BF16)
    return high, mid, low


def dot(a, b, dims):
    return lax.dot_general(a, b, (dims, ((), ())), preferred_element_type=F32)


NN = ((1,), (0,))
NT = ((1,), (1,))
TN = ((0,), (0,))


def onehot_rows(row):
    return (iota((WIDTH, WIDTH), 0) == row).astype(BF16)


def compose(a, b):
    return dot(a, b, NN).astype(BF16)


def tail_table():
    return (iota((WIDTH, WIDTH), 0) + 4 == iota((WIDTH, WIDTH), 1)).astype(BF16)


def unpack(packed):
    full = jnp.concatenate([packed, pltpu.roll(packed, 64, 1)], axis=0)
    return jnp.where(iota(full.shape, 1) < WIDTH, full, 0.0)


def spread_over(x, shape):
    return jnp.broadcast_to(x, shape)


def factor(a_ref, width):
    tile = (8, 128)
    rid = iota(tile, 0)
    count = BLK // 8
    for b in range(PAN // BLK):
        j0 = b * BLK
        lo = j0 // 128 * 128
        wide = width - lo
        tiles = [a_ref[j0 + 8 * t : j0 + 8 * t + 8, lo:width] for t in range(count)]
        for g in range(count):
            c0 = j0 - lo + 8 * g
            cols = [
                [spread_over(tiles[t][:, c0 + k : c0 + k + 1], tile) for t in range(g, count)]
                for k in range(8)
            ]
            for i in range(8):
                inv = 1.0 / spread_over(cols[i][0][i : i + 1, :], tile)
                scale = [c * inv for c in cols[i]]
                scale[0] = jnp.where(rid > i, scale[0], 0.0)
                for k in range(i + 1, 8):
                    s = spread_over(cols[i][0][k : k + 1, :], tile)
                    cols[k] = [c - f * s for c, f in zip(cols[k], scale)]
                row = spread_over(tiles[g][i : i + 1, :], (8, wide))
                for t in range(g, count):
                    f = scale[t - g]
                    tiles[t] = jnp.concatenate(
                        [
                            tiles[t][:, q : q + 128] - f * row[:, q : q + 128]
                            for q in range(0, wide, 128)
                        ],
                        axis=1,
                    )
        rows = jnp.concatenate(tiles, axis=0)
        head = rows[:, 0:128]
        diag = jnp.sum(
            jnp.where(iota(head.shape, 1) == iota(head.shape, 0) + (j0 - lo), head, 0.0),
            axis=1,
            keepdims=True,
        )
        root = lax.rsqrt(diag)
        root = root * (1.5 - 0.5 * diag * root * root)
        rows = rows * root
        a_ref[j0 : j0 + BLK, lo:width] = rows
        r0 = j0 + BLK
        if r0 < PAN:
            nlo = r0 // 128 * 128
            h, m, l = split3(rows[:, nlo - lo :])
            n = PAN - nlo
            left = jnp.concatenate([h, h, m, h, l, m], axis=0)[:, :n]
            right = jnp.concatenate([h, m, h, l, h, m], axis=0)
            done = dot(left, right, TN)
            a_ref[r0:PAN, nlo:width] -= done[r0 - nlo :, :]


def own_columns(own, position):
    p = iota(own.shape, 0)
    t = iota(own.shape, 1)
    kept = jnp.where((t < 4) & (p > t * N + position), 0.0, own)
    return jnp.transpose(kept)[:WIDTH, :]


def rows_of(g_ref, part, first, count, out_ref, more=None):
    for r in range(count):
        for near in range(NEAR):
            for half in range(2):
                at = half * 12 + first + r
                got = g_ref[near // 4][part, near % 4, pl.ds(at, FAR, stride=24), :]
                if more is not None:
                    at = at + near % 4 * FAR * 24
                    got = got + more[near // 4, pl.ds(at, FAR, stride=24), :]
                out_ref[half, pl.ds(r * N + near, FAR, stride=NEAR), :] = got


def joined(r, first, last):
    return jnp.concatenate([r[0, first:last, :], r[1, first:last, :]], axis=1)


def symmetric(g):
    return jnp.where(iota(g.shape, 1) >= iota(g.shape, 0), jnp.transpose(g), g)


def leaf_kernel(
    sc, maps_s, maps_v, leaf, entries, e_ref, ent_ref, ta_ref, tb_ref, stage, big, inv, sems
):
    cube = sc[3]
    chunks = 3840 // 256

    def fetch(j):
        cols = pl.ds(j * 256, 256)
        return pltpu.make_async_copy(leaf.at[0, :, cols], stage.at[:, cols], sems.at[j])

    for j in range(chunks):
        fetch(j).start()

    @pl.loop(0, 72)
    def _(k):
        inv[k] = -1

    @pl.loop(0, KEEP)
    def _(v):
        a0 = maps_s[0, v]
        a1 = maps_s[1, a0]
        a2 = maps_s[2, jnp.maximum(a1, 0)]
        code = jnp.where(a0 < 4, a0, jnp.where(a1 < 4, 4 + a1, 8 + a2))
        inv[code] = v

    t0 = onehot_rows(maps_v[0:1, :])
    t1 = compose(onehot_rows(maps_v[1:2, :]), t0)
    t2 = compose(onehot_rows(maps_v[2:3, :]), t1)
    tt = compose(tail_table(), t2)
    table = jnp.concatenate([tt, t0, t1, t2], axis=0).astype(F32)
    table = jnp.transpose(table).astype(BF16)
    table = jnp.concatenate([table, table, table], axis=0)

    pad = jnp.zeros((WIDTH - KEEP, 256), F32)
    for j in range(chunks):
        fetch(j).wait()
        block = stage[:, j * 256 : (j + 1) * 256]
        block = jnp.concatenate([block, pad], axis=0)
        parts = jnp.concatenate(split3(block), axis=0)
        turned = dot(parts, table, TN)
        big[0, j * 256 : (j + 1) * 256, :] = turned[:, 0:128]
        big[1, j * 256 : (j + 1) * 256, :] = turned[:, 128:256]

    lane = iota((N, 128), 1)
    for h in range(3):
        for k in range(2):
            pieces = []
            for side in range(2):
                v = inv[h * 4 + side * 2 + k]
                got = big[(h + 1) // 2, pl.ds(jnp.maximum(v, 0), N, stride=KEEP), :]
                if (h + 1) % 2 != side:
                    got = pltpu.roll(got, 64, 1)
                pieces.append(jnp.where(v >= 0, got, 0.0))
            e_ref[h, k * N : (k + 1) * N, :] = jnp.where(lane < WIDTH, pieces[0], pieces[1])

    half_lane = iota((N // 2, 128), 1)
    for s in range(8):
        r = jnp.bitwise_xor(s, cube)
        slot = jnp.bitwise_and(r, 2) + jnp.right_shift(r, 2)
        for i in range(8):
            dst = pl.ds(slot * 256 + i, N // 2, stride=8)
            if s * 8 + i < KEEP:
                v = inv[12 + s * 8 + i]
                start = jnp.maximum(v, 0)
                low = big[0, pl.ds(start, N // 2, stride=KEEP), :]
                high = big[0, pl.ds(start + KEEP * N // 2, N // 2, stride=KEEP), :]
                got = jnp.where(half_lane < WIDTH, low, pltpu.roll(high, 64, 1))
                got = jnp.where(v >= 0, got, 0.0)
            else:
                got = jnp.zeros((N // 2, 128), F32)

            @pl.when(jnp.bitwise_and(r, 1) == 0)
            def _():
                ta_ref[dst, :] = got

            @pl.when(jnp.bitwise_and(r, 1) == 1)
            def _():
                tb_ref[dst, :] = got

    p = iota((PAN, PAN), 0)
    order = (iota((PAN, PAN), 1) == (p % N) * 4 + p // N).astype(BF16)
    for h in range(3):
        e = entries[sc[h]]
        e3 = split3(e)
        placed = dot(order, e3[0], NT) + dot(order, e3[1], NT) + dot(order, e3[2], NT)
        ent_ref[h] = jnp.concatenate([placed[:128], placed[128:]], axis=1)


def pick_kernel(sc, maps_v, e, ent, x_ref, xp_ref, send_ref):
    core = sc[5]
    x = jnp.right_shift(sc[3], 1)
    x0 = e[0, 0] + e[1, 0] + ent[0]
    x1 = e[0, 1] + e[1, 1] + jnp.where(jnp.bitwise_and(x, 1) == 0, ent[1], 0.0)
    x2 = e[0, 2] + e[1, 2] + jnp.where(x == 0, ent[2], 0.0)
    x_ref[...] = x0
    xp_ref[0], xp_ref[1] = x1, x2
    m1 = onehot_rows(maps_v[1:2, :])
    m2 = onehot_rows(maps_v[2:3, :])
    m21 = compose(m2, m1)
    eye = (iota((WIDTH, WIDTH), 0) == iota((WIDTH, WIDTH), 1)).astype(BF16)

    def first4(tables):
        four = [x.astype(F32)[:8] for x in tables]
        while len(four) < 3:
            four.append(jnp.zeros_like(four[0]))
        return jnp.concatenate(four, axis=0)

    zero = jnp.zeros((8, WIDTH), F32)
    s0 = jnp.where(core == 0, first4([eye, m1, m21]), 0.0)
    s1 = jnp.where(core == 1, first4([eye, m2]), 0.0)
    s2 = jnp.where(
        core == 1, jnp.concatenate([zero, zero, eye.astype(F32)[:8]], axis=0), 0.0
    )
    z = jnp.zeros((24, PAN), F32)
    for s, x in ((s0, x0), (s1, x1), (s2, x2)):
        full = jnp.concatenate([x, pltpu.roll(x, 64, 1)], axis=0)[:, :WIDTH]
        table = s.astype(BF16)
        h, m, l = split3(full)
        z = z + (dot(table, h, NT) + dot(table, m, NT) + dot(table, l, NT))
    rows = jnp.concatenate([z[0:4], z[8:12], z[16:20]], axis=0)
    rows = jnp.concatenate([rows[:, :128], rows[:, 128:]], axis=0)
    for k in range(FAR):
        send_ref[k] = rows


def level0_kernel(sc, maps_v, ga, gb, x, ta, tr, f_ref, v_ref, tk_ref, ts_ref, a, r):
    tk_ref[...] = ta[0:512, :] + tr[0:512, :]
    ts_ref[...] = ta[512:1024, :] + tr[512:1024, :]
    rows_of((ga, gb), 0, 0, 12, r)
    a[:, 0:256] = symmetric(joined(r, 0, 256))
    a[:, 256:768] = jnp.transpose(joined(r, 256, 768))
    a[:, 768:896] = unpack(x[...])
    factor(a, 896)
    own = a[:, 768:896]
    f_ref[...] = own_columns(own, sc[4])
    m1 = onehot_rows(maps_v[1:2, :])
    v_ref[:, 0:512] = a[:, 256:768].astype(BF16)
    moved = dot(own[:, :WIDTH].astype(BF16), m1, NT)
    v_ref[:, 512:640] = jnp.concatenate([moved, jnp.zeros_like(moved)], axis=1).astype(BF16)


def level1_kernel(
    sc, maps_v, ga, gb, xp, cross, more, v0, v0s, f_ref, d_ref, half_ref, a, r
):
    rows_of((ga, gb), 1, 0, 12, r, more)
    a[:, 0:256] = symmetric(joined(r, 0, 256))
    a[:, 256:512] = jnp.transpose(joined(r, 256, 512))
    a[:, 512:640] = unpack(xp[0] + cross[768:896, :])
    mine, other = v0[...], v0s[...]
    a[...] -= dot(mine[:, 0:256], mine, TN) + dot(other[:, 0:256], other, TN)
    factor(a, 640)
    own = a[:, 512:640]
    f_ref[...] = own_columns(own, sc[4])
    m2 = onehot_rows(maps_v[2:3, :])
    moved = [
        dot(mine[:, 512 : 512 + WIDTH], m2, NT).astype(BF16),
        dot(other[:, 512 : 512 + WIDTH], m2, NT).astype(BF16),
        dot(own[:, :WIDTH].astype(BF16), m2, NT).astype(BF16),
    ]
    cols = [mine[:, 256:512], other[:, 256:512], a[:, 256:512].astype(BF16)]
    zero = jnp.zeros((PAN, WIDTH), F32)
    right0 = [jnp.concatenate([c.astype(F32), m.astype(F32), zero], axis=1) for c, m in zip(cols, moved)]
    total = jnp.zeros((PAN, 384), F32)
    for c, right in zip(cols, right0):
        total = total + dot(c, right.astype(BF16), TN)
    d_ref[:, 0:256] = total[:, 0:256] - symmetric(joined(r, 512, 768))
    own2 = unpack(xp[1] + cross[896:1024, :])
    total = total[:, 256:384] - own2
    d_ref[:, 256:384] = jnp.concatenate(
        [total[:, :WIDTH], moved[0].astype(F32)], axis=1
    )
    d_ref[:, 384:512] = jnp.concatenate(
        [moved[1].astype(F32), moved[2].astype(F32)], axis=1
    )
    first = pl.multiple_of(sc[5] * 128, 128)
    half_ref[...] = d_ref[pl.ds(first, 128), :]


def level2_kernel(
    sc, d, ds, f0, f1, tk, tr, f_ref, send_ref, vw_ref, tk_ref, ts_ref, a
):
    tk_ref[...] = tk[0:256, :] + tr[0:256, :]
    ts_ref[...] = tk[256:512, :] + tr[256:512, :]
    sib = jnp.concatenate([ds[0], ds[1]], axis=0)
    mine = d[...]
    sub = mine[:, 0:384] + sib[:, 0:384]
    a[:, 0:256] = -sub[:, 0:256]
    a[:, 256:384] = jnp.where(iota((PAN, 128), 1) < WIDTH, -sub[:, 256:384], 0.0)
    factor(a, 384)
    own = a[:, 256:384]
    f_ref[0] = f0[...]
    f_ref[1] = f1[...]
    f_ref[2] = own_columns(own, sc[4])
    pieces = [
        m[:, first : first + WIDTH].astype(BF16)
        for m in (mine, sib)
        for first in (320, 384, 448)
    ]
    pieces.append(own[:, :WIDTH].astype(BF16))
    first = 4 + 8 * sc[3]
    pick = (iota((8, WIDTH), 0) + first == iota((8, WIDTH), 1)).astype(BF16)
    thick = jnp.concatenate([dot(pick, v, NT) for v in pieces], axis=0)
    thick = jnp.concatenate([thick[:, :128], thick[:, 128:]], axis=0).astype(BF16)
    for k in range(FAR):
        send_ref[k] = thick
    src = iota((WIDTH, 128), 0)
    dst = iota((WIDTH, 128), 1)
    low = (src == dst + 4).astype(BF16)
    low = jnp.where(dst < KEEP, low, jnp.zeros_like(low))
    high = ((src == dst - 60) & (dst >= WIDTH)).astype(BF16)
    for n, v in enumerate(pieces):
        vw_ref[0, n * PAN : (n + 1) * PAN, :] = dot(v, low, NN).astype(BF16)
        vw_ref[1, n * PAN : (n + 1) * PAN, :] = dot(v, high, NN).astype(BF16)


def top_kernel(tk, tr, got, vw, out, big):
    for near in range(NEAR):
        for far in range(FAR):
            block = got[near, far].astype(F32)
            d = far * NEAR + near
            for n in range(7):
                for half in range(2):
                    first = half * 56 + n * 8
                    big[d * 8 : d * 8 + 8, (n * 2 + half) * 128 : (n * 2 + half + 1) * 128] = (
                        block[first : first + 8, :]
                    )
    low = dot(big[0:256, :].astype(BF16), vw[0], NN)
    high = dot(big[256:512, :].astype(BF16), vw[1], NN)
    piece = tk[...] + tr[...] - (low + high)
    last = piece[248:256, :]
    lane = iota((8, 128), 1)
    for t in range(31):
        rows = piece[8 * t : 8 * t + 8, :]
        if t < 16:
            one = pltpu.roll(last, (60 - 8 * t) % 128, 1)
            two = pltpu.roll(last, (120 - 8 * t) % 128, 1)
            rows = jnp.where(
                lane >= 124, two, jnp.where((lane >= 60) & (lane < 64), one, rows)
            )
        out[8 * t : 8 * t + 8, :] = rows


def last_kernel(t, out):
    lane = iota((8, 128), 1)
    ends = []
    for s in range(8):
        end = jnp.zeros((8, 128), F32)
        for k in range(16):
            rows = t[s, 8 * k : 8 * k + 8, :]
            one = pltpu.roll(rows, (8 * k - 60) % 128, 1)
            two = pltpu.roll(rows, (8 * k - 120) % 128, 1)
            end = jnp.where(lane // 4 == 2 * k, one, jnp.where(lane // 4 == 2 * k + 1, two, end))
        ends.append(end)
    for d in range(N // 2):
        if d < N // 2 - 1:
            block = jnp.concatenate([t[s, d * 8 : d * 8 + 8, :] for s in range(8)], axis=0)
        else:
            block = jnp.concatenate(ends, axis=0)
        turned = jnp.transpose(block)
        out[:, d * KEEP : (d + 1) * KEEP] = turned[0:KEEP, 0:KEEP]
        d2 = d + N // 2
        out[:, d2 * KEEP : (d2 + 1) * KEEP] = turned[WIDTH : WIDTH + KEEP, 0:KEEP]


def call(kernel, specs, outs, scratch=(), flops=10**8, name=None):
    return pl.pallas_call(
        kernel,
        in_specs=specs,
        out_specs=[VMEM] * len(outs),
        out_shape=[jax.ShapeDtypeStruct(s, t) for s, t in outs],
        scratch_shapes=list(scratch),
        compiler_params=pltpu.CompilerParams(vmem_limit_bytes=48 * 2**20),
        cost_estimate=pl.CostEstimate(flops=flops, bytes_accessed=4 * 10**6, transcendentals=0),
        name=name,
    )


def crossed(value, mask):
    return lax.ppermute(value, "cube", [(c, c ^ mask) for c in range(8)])


def spread(value, axis_groups):
    return lax.all_to_all(value, "front", 0, 0, axis_index_groups=axis_groups, tiled=True)


def gather_front(sent, rows):
    lanes = sent.shape[-1]
    got = spread(sent.reshape(FAR * rows, lanes), FAR_GROUPS)
    copies = jnp.broadcast_to(got[None], (NEAR, FAR * rows, lanes))
    got = spread(copies.reshape(NEAR * FAR * rows, lanes), NEAR_GROUPS)
    return got.reshape(NEAR, FAR * rows, lanes)


def on_device(leaf_blocks, front_entries, child_maps):
    position = lax.axis_index("front")
    cube = lax.axis_index("cube")
    core = cube & 1
    nodes = [jnp.right_shift(cube + 8, h + 1) for h in range(3)]
    sides = [jnp.right_shift(cube, h) & 1 for h in range(3)]
    sc = jnp.stack(
        [n - 1 for n in nodes] + [cube, position, core, jnp.right_shift(cube, 2), cube * 0]
    ).astype(jnp.int32)
    picked = [
        lax.dynamic_slice(child_maps, (n - 1, s, 0), (1, 1, KEEP)).reshape(KEEP)
        for n, s in zip(nodes, sides)
    ]
    none = jnp.full((4,), -1, jnp.int32)
    maps = jnp.stack(
        [
            jnp.concatenate([picked[0], none]),
            jnp.concatenate([none, picked[1]]),
            jnp.concatenate([none, picked[2]]),
        ]
    )

    e, ent, ta, tb = call(
        leaf_kernel,
        [SMEM, SMEM, VMEM, pl.BlockSpec(memory_space=pltpu.HBM), VMEM],
        [((3, 128, 128), F32), ((3, 128, 128), F32), ((1024, 128), F32), ((1024, 128), F32)],
        [
            pltpu.VMEM((KEEP, 3840), F32),
            pltpu.VMEM((2, 3840, 128), F32),
            pltpu.SMEM((128,), jnp.int32),
            pltpu.SemaphoreType.DMA((15,)),
        ],
        name="leaf",
    )(sc, maps, maps, leaf_blocks, front_entries)

    both = lax.all_gather(e, "cube", axis_index_groups=CORE_GROUPS, axis=0)
    x, xp, sent = call(
        pick_kernel,
        [SMEM] + [VMEM] * 3,
        [((128, 128), F32), ((2, 128, 128), F32), ((FAR, 24, 128), F32)],
        name="pick",
    )(sc, maps, both, ent)
    g = gather_front(sent, 24)
    ga, gb = [
        lax.all_gather(part, "cube", axis_index_groups=CORE_GROUPS, axis=0)
        for part in (g[:4], g[4:])
    ]

    mine = jnp.where(core == 0, ga[1], gb[1]).reshape(768, 128)
    cross = crossed(jnp.concatenate([mine, xp.reshape(256, 128)], axis=0), 2)

    tr = crossed(tb, 1)
    f0, v0, tk, ts = call(
        level0_kernel,
        [SMEM] + [VMEM] * 6,
        [((WIDTH, PAN), F32), ((PAN, 640), BF16), ((512, 128), F32), ((512, 128), F32)],
        [pltpu.VMEM((PAN, 896), F32), pltpu.VMEM((2, 768, 128), F32)],
        flops=10**9,
        name="level0",
    )(sc, maps, ga, gb, x, ta, tr)
    v0s, ts = lax.optimization_barrier((crossed(v0, 2), ts))
    tr = crossed(ts, 2)
    more = lax.all_gather(cross[:768], "cube", axis_index_groups=CORE_GROUPS, axis=0)
    f1, d1, half = call(
        level1_kernel,
        [SMEM] + [VMEM] * 8,
        [((WIDTH, PAN), F32), ((PAN, 512), F32), ((128, 512), F32)],
        [pltpu.VMEM((PAN, 640), F32), pltpu.VMEM((2, 768, 128), F32)],
        flops=10**9,
        name="level1",
    )(sc, maps, ga, gb, xp, cross, more, v0, v0s)
    half, tr = lax.optimization_barrier((half, tr))
    d1s = lax.all_gather(crossed(half, 4), "cube", axis_index_groups=CORE_GROUPS, axis=0)
    factors, thick, vw, tk, ts = call(
        level2_kernel,
        [SMEM] + [VMEM] * 6,
        [
            ((3, WIDTH, PAN), F32),
            ((FAR, 112, 128), BF16),
            ((2, 7 * PAN, 128), BF16),
            ((256, 128), F32),
            ((256, 128), F32),
        ],
        [pltpu.VMEM((PAN, 384), F32)],
        flops=10**9,
        name="level2",
    )(sc, d1, d1s, f0, f1, tk, tr)
    tr = crossed(ts, 4)
    thick = gather_front(thick, 112).reshape(NEAR, FAR, 112, 128)
    (piece,) = call(
        top_kernel,
        [VMEM] * 4,
        [((248, 128), F32)],
        [pltpu.VMEM((512, 7 * PAN), F32)],
        name="top",
    )(tk, tr, thick, vw)
    pieces = lax.all_gather(piece, "cube", axis=0)
    (top,) = call(last_kernel, [VMEM], [((KEEP, KEEP * N), F32)], name="last")(pieces)
    return factors[None], top


def solution(mesh):
    in_specs = (P("cube", "front", None), P(None, "front", None), P())
    out_specs = (P("cube", None, "front", None), P("front", None))
    return jax.shard_map(
        on_device, mesh=mesh, in_specs=in_specs, out_specs=out_specs, check_vma=False
    )
```

```python
import functools

import jax
import jax.numpy as jnp
from jax import lax
from jax.experimental import pallas as pl
from jax.experimental.pallas import tpu as pltpu
from jax.sharding import PartitionSpec as P

F32 = jnp.float32
BF16 = jnp.bfloat16
HIGH = lax.Precision.HIGHEST

N = 64
FAR, NEAR = 8, 8
WIDTH = 64
KEEP = 60
PAN = 256
BLK = 32

FAR_GROUPS = [[NEAR * far + near for far in range(FAR)] for near in range(NEAR)]
NEAR_GROUPS = [[NEAR * far + near for near in range(NEAR)] for far in range(FAR)]
CORE_GROUPS = [[0, 1], [2, 3], [4, 5], [6, 7]]

VMEM = pl.BlockSpec(memory_space=pltpu.VMEM)
SMEM = pl.BlockSpec(memory_space=pltpu.SMEM)


def iota(shape, dim):
    return lax.broadcasted_iota(jnp.int32, shape, dim)


def split3(x):
    high = x.astype(BF16)
    rest = x - high.astype(F32)
    mid = rest.astype(BF16)
    low = (rest - mid.astype(F32)).astype(BF16)
    return high, mid, low


def dot(a, b, dims):
    return lax.dot_general(a, b, (dims, ((), ())), preferred_element_type=F32)


NN = ((1,), (0,))
NT = ((1,), (1,))
TN = ((0,), (0,))


def onehot_rows(row):
    return (iota((WIDTH, WIDTH), 0) == row).astype(BF16)


def compose(a, b):
    return dot(a, b, NN).astype(BF16)


def tail_table():
    return (iota((WIDTH, WIDTH), 0) + 4 == iota((WIDTH, WIDTH), 1)).astype(BF16)


def unpack(packed):
    full = jnp.concatenate([packed, pltpu.roll(packed, 64, 1)], axis=0)
    return jnp.where(iota(full.shape, 1) < WIDTH, full, 0.0)


def spread_over(x, shape):
    return jnp.broadcast_to(x, shape)


def factor(a_ref, width):
    tile = (8, 128)
    rid = iota(tile, 0)
    count = BLK // 8
    for b in range(PAN // BLK):
        j0 = b * BLK
        lo = j0 // 128 * 128
        wide = width - lo
        tiles = [a_ref[j0 + 8 * t : j0 + 8 * t + 8, lo:width] for t in range(count)]
        for g in range(count):
            c0 = j0 - lo + 8 * g
            cols = [
                [spread_over(tiles[t][:, c0 + k : c0 + k + 1], tile) for t in range(g, count)]
                for k in range(8)
            ]
            for i in range(8):
                inv = 1.0 / spread_over(cols[i][0][i : i + 1, :], tile)
                scale = [c * inv for c in cols[i]]
                scale[0] = jnp.where(rid > i, scale[0], 0.0)
                for k in range(i + 1, 8):
                    s = spread_over(cols[i][0][k : k + 1, :], tile)
                    cols[k] = [c - f * s for c, f in zip(cols[k], scale)]
                row = spread_over(tiles[g][i : i + 1, :], (8, wide))
                for t in range(g, count):
                    f = scale[t - g]
                    tiles[t] = jnp.concatenate(
                        [
                            tiles[t][:, q : q + 128] - f * row[:, q : q + 128]
                            for q in range(0, wide, 128)
                        ],
                        axis=1,
                    )
        rows = jnp.concatenate(tiles, axis=0)
        head = rows[:, 0:128]
        diag = jnp.sum(
            jnp.where(iota(head.shape, 1) == iota(head.shape, 0) + (j0 - lo), head, 0.0),
            axis=1,
            keepdims=True,
        )
        root = lax.rsqrt(diag)
        root = root * (1.5 - 0.5 * diag * root * root)
        rows = rows * root
        a_ref[j0 : j0 + BLK, lo:width] = rows
        r0 = j0 + BLK
        if r0 < PAN:
            nlo = r0 // 128 * 128
            h, m, l = split3(rows[:, nlo - lo :])
            n = PAN - nlo
            left = jnp.concatenate([h, h, m, h, l, m], axis=0)[:, :n]
            right = jnp.concatenate([h, m, h, l, h, m], axis=0)
            done = dot(left, right, TN)
            a_ref[r0:PAN, nlo:width] -= done[r0 - nlo :, :]


def own_columns(own, position):
    p = iota(own.shape, 0)
    t = iota(own.shape, 1)
    kept = jnp.where((t < 4) & (p > t * N + position), 0.0, own)
    return jnp.transpose(kept)[:WIDTH, :]


def rows_of(g_ref, part, first, count, out_ref, more=None):
    for r in range(count):
        for near in range(NEAR):
            for half in range(2):
                at = half * 12 + first + r
                got = g_ref[near // 4][part, near % 4, pl.ds(at, FAR, stride=24), :]
                if more is not None:
                    at = at + near % 4 * FAR * 24
                    got = got + more[near // 4, pl.ds(at, FAR, stride=24), :]
                out_ref[half, pl.ds(r * N + near, FAR, stride=NEAR), :] = got


def joined(r, first, last):
    return jnp.concatenate([r[0, first:last, :], r[1, first:last, :]], axis=1)


def symmetric(g):
    return jnp.where(iota(g.shape, 1) >= iota(g.shape, 0), jnp.transpose(g), g)


def leaf_kernel(
    sc, maps_s, maps_v, leaf, entries, e_ref, ent_ref, t_ref, big, inv
):
    cube = sc[3]
    chunks = 3840 // 256

    @pl.loop(0, 72)
    def _(k):
        inv[k] = -1

    @pl.loop(0, KEEP, unroll=12)
    def _(v):
        a0 = maps_s[0, v]
        a1 = maps_s[1, a0]
        a2 = maps_s[2, jnp.maximum(a1, 0)]
        code = jnp.where(a0 < 4, a0, jnp.where(a1 < 4, 4 + a1, 8 + a2))
        inv[code] = v

    t0 = onehot_rows(maps_v[0:1, :])
    t1 = compose(onehot_rows(maps_v[1:2, :]), t0)
    t2 = compose(onehot_rows(maps_v[2:3, :]), t1)
    tt = compose(tail_table(), t2)
    table = jnp.concatenate([tt, t0, t1, t2], axis=0).astype(F32)
    table = jnp.transpose(table).astype(BF16)
    table = jnp.concatenate([table, table, table], axis=0)

    pad = jnp.zeros((WIDTH - KEEP, 256), F32)
    for j in range(chunks):
        block = leaf[0, :, j * 256 : (j + 1) * 256]
        block = jnp.concatenate([block, pad], axis=0)
        parts = jnp.concatenate(split3(block), axis=0)
        turned = dot(parts, table, TN)
        big[0, j * 256 : (j + 1) * 256, :] = turned[:, 0:128]
        big[1, j * 256 : (j + 1) * 256, :] = turned[:, 128:256]

    lane = iota((N, 128), 1)
    for h in range(3):
        for k in range(2):
            pieces = []
            for side in range(2):
                v = inv[h * 4 + side * 2 + k]
                got = big[(h + 1) // 2, pl.ds(jnp.maximum(v, 0), N, stride=KEEP), :]
                if (h + 1) % 2 != side:
                    got = pltpu.roll(got, 64, 1)
                pieces.append(jnp.where(v >= 0, got, 0.0))
            e_ref[h, k * N : (k + 1) * N, :] = jnp.where(lane < WIDTH, pieces[0], pieces[1])

    half_lane = iota((N // 2, 128), 1)
    for s in range(8):
        r = jnp.bitwise_xor(s, cube)
        slot = jnp.bitwise_and(r, 1) * 4 + jnp.bitwise_and(r, 2) + jnp.right_shift(r, 2)
        for i in range(8):
            dst = pl.ds(slot * 256 + i, N // 2, stride=8)
            if s * 8 + i < KEEP:
                v = inv[12 + s * 8 + i]
                start = jnp.maximum(v, 0)
                low = big[0, pl.ds(start, N // 2, stride=KEEP), :]
                high = big[0, pl.ds(start + KEEP * N // 2, N // 2, stride=KEEP), :]
                got = jnp.where(half_lane < WIDTH, low, pltpu.roll(high, 64, 1))
                got = jnp.where(v >= 0, got, 0.0)
            else:
                got = jnp.zeros((N // 2, 128), F32)

            t_ref[dst, :] = got

    p = iota((PAN, PAN), 0)
    order = (iota((PAN, PAN), 1) == (p % N) * 4 + p // N).astype(BF16)
    for h in range(3):
        e = entries[sc[h]]
        e3 = split3(e)
        placed = dot(order, e3[0], NT) + dot(order, e3[1], NT) + dot(order, e3[2], NT)
        ent_ref[h] = jnp.concatenate([placed[:128], placed[128:]], axis=1)


def pick_kernel(sc, maps_v, e, ent, x_ref, xp_ref, send_ref):
    core = sc[5]
    x = jnp.right_shift(sc[3], 1)
    x0 = e[0, 0] + e[1, 0] + ent[0]
    x1 = e[0, 1] + e[1, 1] + jnp.where(jnp.bitwise_and(x, 1) == 0, ent[1], 0.0)
    x2 = e[0, 2] + e[1, 2] + jnp.where(x == 0, ent[2], 0.0)
    x_ref[...] = x0
    xp_ref[0], xp_ref[1] = x1, x2
    m1 = onehot_rows(maps_v[1:2, :])
    m2 = onehot_rows(maps_v[2:3, :])
    m21 = compose(m2, m1)
    eye = (iota((WIDTH, WIDTH), 0) == iota((WIDTH, WIDTH), 1)).astype(BF16)

    def first4(tables):
        four = [x.astype(F32)[:8] for x in tables]
        while len(four) < 3:
            four.append(jnp.zeros_like(four[0]))
        return jnp.concatenate(four, axis=0)

    zero = jnp.zeros((8, WIDTH), F32)
    s0 = jnp.where(core == 0, first4([eye, m1, m21]), 0.0)
    s1 = jnp.where(core == 1, first4([eye, m2]), 0.0)
    s2 = jnp.where(
        core == 1, jnp.concatenate([zero, zero, eye.astype(F32)[:8]], axis=0), 0.0
    )
    z = jnp.zeros((24, PAN), F32)
    for s, x in ((s0, x0), (s1, x1), (s2, x2)):
        full = jnp.concatenate([x, pltpu.roll(x, 64, 1)], axis=0)[:, :WIDTH]
        table = s.astype(BF16)
        h, m, l = split3(full)
        z = z + (dot(table, h, NT) + dot(table, m, NT) + dot(table, l, NT))
    rows = jnp.concatenate([z[0:4], z[8:12], z[16:20]], axis=0)
    rows = jnp.concatenate([rows[:, :128], rows[:, 128:]], axis=0)
    for k in range(FAR):
        send_ref[k] = rows


def level0_kernel(sc, maps_v, ga, gb, x, ta, tr, f_ref, v_ref, tk_ref, ts_ref, a, r):
    tk_ref[...] = ta[0:512, :] + tr[0:512, :]
    ts_ref[...] = ta[512:1024, :] + tr[512:1024, :]
    rows_of((ga, gb), 0, 0, 12, r)
    a[:, 0:256] = symmetric(joined(r, 0, 256))
    a[:, 256:768] = jnp.transpose(joined(r, 256, 768))
    a[:, 768:896] = unpack(x[...])
    factor(a, 896)
    own = a[:, 768:896]
    f_ref[...] = own_columns(own, sc[4])
    m1 = onehot_rows(maps_v[1:2, :])
    v_ref[:, 0:512] = a[:, 256:768].astype(BF16)
    moved = dot(own[:, :WIDTH].astype(BF16), m1, NT)
    v_ref[:, 512:640] = jnp.concatenate([moved, jnp.zeros_like(moved)], axis=1).astype(BF16)


def level1_kernel(
    sc, maps_v, ga, gb, xp, cross, more, v0, v0s, f_ref, d_ref, half_ref, a, r
):
    rows_of((ga, gb), 1, 0, 12, r, more)
    a[:, 0:256] = symmetric(joined(r, 0, 256))
    a[:, 256:512] = jnp.transpose(joined(r, 256, 512))
    a[:, 512:640] = unpack(xp[0] + cross[768:896, :])
    mine, other = v0[...], v0s[...]
    a[...] -= dot(mine[:, 0:256], mine, TN) + dot(other[:, 0:256], other, TN)
    factor(a, 640)
    own = a[:, 512:640]
    f_ref[...] = own_columns(own, sc[4])
    m2 = onehot_rows(maps_v[2:3, :])
    moved = [
        dot(mine[:, 512 : 512 + WIDTH], m2, NT).astype(BF16),
        dot(other[:, 512 : 512 + WIDTH], m2, NT).astype(BF16),
        dot(own[:, :WIDTH].astype(BF16), m2, NT).astype(BF16),
    ]
    cols = [mine[:, 256:512], other[:, 256:512], a[:, 256:512].astype(BF16)]
    zero = jnp.zeros((PAN, WIDTH), F32)
    right0 = [jnp.concatenate([c.astype(F32), m.astype(F32), zero], axis=1) for c, m in zip(cols, moved)]
    total = jnp.zeros((PAN, 384), F32)
    for c, right in zip(cols, right0):
        total = total + dot(c, right.astype(BF16), TN)
    d_ref[:, 0:256] = total[:, 0:256] - symmetric(joined(r, 512, 768))
    own2 = unpack(xp[1] + cross[896:1024, :])
    total = total[:, 256:384] - own2
    d_ref[:, 256:384] = jnp.concatenate(
        [total[:, :WIDTH], moved[0].astype(F32)], axis=1
    )
    d_ref[:, 384:512] = jnp.concatenate(
        [moved[1].astype(F32), moved[2].astype(F32)], axis=1
    )
    first = pl.multiple_of(sc[5] * 128, 128)
    half_ref[...] = d_ref[pl.ds(first, 128), :]


def level2_kernel(
    sc, d, ds, f0, f1, tk, tr, f_ref, send_ref, vw_ref, tk_ref, ts_ref, a
):
    tk_ref[...] = tk[0:256, :] + tr[0:256, :]
    ts_ref[...] = tk[256:512, :] + tr[256:512, :]
    sib = jnp.concatenate([ds[0], ds[1]], axis=0)
    mine = d[...]
    sub = mine[:, 0:384] + sib[:, 0:384]
    a[:, 0:256] = -sub[:, 0:256]
    a[:, 256:384] = jnp.where(iota((PAN, 128), 1) < WIDTH, -sub[:, 256:384], 0.0)
    factor(a, 384)
    own = a[:, 256:384]
    f_ref[0] = f0[...]
    f_ref[1] = f1[...]
    f_ref[2] = own_columns(own, sc[4])
    pieces = [
        m[:, first : first + WIDTH].astype(BF16)
        for m in (mine, sib)
        for first in (320, 384, 448)
    ]
    pieces.append(own[:, :WIDTH].astype(BF16))
    first = 4 + 8 * sc[3]
    pick = (iota((8, WIDTH), 0) + first == iota((8, WIDTH), 1)).astype(BF16)
    thick = jnp.concatenate([dot(pick, v, NT) for v in pieces], axis=0)
    thick = jnp.concatenate([thick[:, :128], thick[:, 128:]], axis=0).astype(BF16)
    for k in range(FAR):
        send_ref[k] = thick
    src = iota((WIDTH, 128), 0)
    dst = iota((WIDTH, 128), 1)
    low = (src == dst + 4).astype(BF16)
    low = jnp.where(dst < KEEP, low, jnp.zeros_like(low))
    high = ((src == dst - 60) & (dst >= WIDTH)).astype(BF16)
    for n, v in enumerate(pieces):
        vw_ref[0, n * PAN : (n + 1) * PAN, :] = dot(v, low, NN).astype(BF16)
        vw_ref[1, n * PAN : (n + 1) * PAN, :] = dot(v, high, NN).astype(BF16)


def top_kernel(tk, tr, got, vw, out, big):
    for near in range(NEAR):
        for far in range(FAR):
            block = got[near, far].astype(F32)
            d = far * NEAR + near
            for n in range(7):
                for half in range(2):
                    first = half * 56 + n * 8
                    big[d * 8 : d * 8 + 8, (n * 2 + half) * 128 : (n * 2 + half + 1) * 128] = (
                        block[first : first + 8, :]
                    )
    low = dot(big[0:256, :].astype(BF16), vw[0], NN)
    high = dot(big[256:512, :].astype(BF16), vw[1], NN)
    piece = tk[...] + tr[...] - (low + high)
    last = piece[248:256, :]
    lane = iota((8, 128), 1)
    for t in range(31):
        rows = piece[8 * t : 8 * t + 8, :]
        if t < 16:
            one = pltpu.roll(last, (60 - 8 * t) % 128, 1)
            two = pltpu.roll(last, (120 - 8 * t) % 128, 1)
            rows = jnp.where(
                lane >= 124, two, jnp.where((lane >= 60) & (lane < 64), one, rows)
            )
        out[8 * t : 8 * t + 8, :] = rows


def last_kernel(t, out):
    lane = iota((8, 128), 1)
    ends = []
    for s in range(8):
        end = jnp.zeros((8, 128), F32)
        for k in range(16):
            rows = t[s, 8 * k : 8 * k + 8, :]
            one = pltpu.roll(rows, (8 * k - 60) % 128, 1)
            two = pltpu.roll(rows, (8 * k - 120) % 128, 1)
            end = jnp.where(lane // 4 == 2 * k, one, jnp.where(lane // 4 == 2 * k + 1, two, end))
        ends.append(end)
    for d in range(N // 2):
        if d < N // 2 - 1:
            block = jnp.concatenate([t[s, d * 8 : d * 8 + 8, :] for s in range(8)], axis=0)
        else:
            block = jnp.concatenate(ends, axis=0)
        turned = jnp.transpose(block)
        out[:, d * KEEP : (d + 1) * KEEP] = turned[0:KEEP, 0:KEEP]
        d2 = d + N // 2
        out[:, d2 * KEEP : (d2 + 1) * KEEP] = turned[WIDTH : WIDTH + KEEP, 0:KEEP]


def call(kernel, specs, outs, scratch=(), flops=10**8, name=None):
    return pl.pallas_call(
        kernel,
        in_specs=specs,
        out_specs=[VMEM] * len(outs),
        out_shape=[jax.ShapeDtypeStruct(s, t) for s, t in outs],
        scratch_shapes=list(scratch),
        compiler_params=pltpu.CompilerParams(vmem_limit_bytes=48 * 2**20),
        cost_estimate=pl.CostEstimate(flops=flops, bytes_accessed=4 * 10**6, transcendentals=0),
        name=name,
    )


def crossed(value, mask):
    return lax.ppermute(value, "cube", [(c, c ^ mask) for c in range(8)])


def spread(value, axis_groups):
    return lax.all_to_all(value, "front", 0, 0, axis_index_groups=axis_groups, tiled=True)


def gather_front(sent, rows):
    lanes = sent.shape[-1]
    got = spread(sent.reshape(FAR * rows, lanes), FAR_GROUPS)
    copies = jnp.broadcast_to(got[None], (NEAR, FAR * rows, lanes))
    got = spread(copies.reshape(NEAR * FAR * rows, lanes), NEAR_GROUPS)
    return got.reshape(NEAR, FAR * rows, lanes)


def on_device(leaf_blocks, front_entries, child_maps):
    position = lax.axis_index("front")
    cube = lax.axis_index("cube")
    core = cube & 1
    nodes = [jnp.right_shift(cube + 8, h + 1) for h in range(3)]
    sides = [jnp.right_shift(cube, h) & 1 for h in range(3)]
    sc = jnp.stack(
        [n - 1 for n in nodes] + [cube, position, core, jnp.right_shift(cube, 2), cube * 0]
    ).astype(jnp.int32)
    picked = [
        lax.dynamic_slice(child_maps, (n - 1, s, 0), (1, 1, KEEP)).reshape(KEEP)
        for n, s in zip(nodes, sides)
    ]
    none = jnp.full((4,), -1, jnp.int32)
    maps = jnp.stack(
        [
            jnp.concatenate([picked[0], none]),
            jnp.concatenate([none, picked[1]]),
            jnp.concatenate([none, picked[2]]),
        ]
    )

    e, ent, t = call(
        leaf_kernel,
        [SMEM, SMEM, VMEM, VMEM, VMEM],
        [((3, 128, 128), F32), ((3, 128, 128), F32), ((2048, 128), F32)],
        [
            pltpu.VMEM((2, 3840, 128), F32),
            pltpu.SMEM((128,), jnp.int32),
        ],
        name="leaf",
    )(sc, maps, maps, leaf_blocks, front_entries)

    both = lax.all_gather(e, "cube", axis_index_groups=CORE_GROUPS, axis=0)
    x, xp, sent = call(
        pick_kernel,
        [SMEM] + [VMEM] * 3,
        [((128, 128), F32), ((2, 128, 128), F32), ((FAR, 24, 128), F32)],
        name="pick",
    )(sc, maps, both, ent)
    g = gather_front(sent, 24)
    ga, gb = [
        lax.all_gather(part, "cube", axis_index_groups=CORE_GROUPS, axis=0)
        for part in (g[:4], g[4:])
    ]

    mine = jnp.where(core == 0, ga[1], gb[1]).reshape(768, 128)
    cross = crossed(jnp.concatenate([mine, xp.reshape(256, 128)], axis=0), 2)

    tr = crossed(t[1024:], 1)
    f0, v0, tk, ts = call(
        level0_kernel,
        [SMEM] + [VMEM] * 6,
        [((WIDTH, PAN), F32), ((PAN, 640), BF16), ((512, 128), F32), ((512, 128), F32)],
        [pltpu.VMEM((PAN, 896), F32), pltpu.VMEM((2, 768, 128), F32)],
        flops=10**9,
        name="level0",
    )(sc, maps, ga, gb, x, t, tr)
    v0s, ts = lax.optimization_barrier((crossed(v0, 2), ts))
    tr = crossed(ts, 2)
    more = lax.all_gather(cross[:768], "cube", axis_index_groups=CORE_GROUPS, axis=0)
    f1, d1, half = call(
        level1_kernel,
        [SMEM] + [VMEM] * 8,
        [((WIDTH, PAN), F32), ((PAN, 512), F32), ((128, 512), F32)],
        [pltpu.VMEM((PAN, 640), F32), pltpu.VMEM((2, 768, 128), F32)],
        flops=10**9,
        name="level1",
    )(sc, maps, ga, gb, xp, cross, more, v0, v0s)
    half, tr = lax.optimization_barrier((half, tr))
    d1s = lax.all_gather(crossed(half, 4), "cube", axis_index_groups=CORE_GROUPS, axis=0)
    factors, thick, vw, tk, ts = call(
        level2_kernel,
        [SMEM] + [VMEM] * 6,
        [
            ((3, WIDTH, PAN), F32),
            ((FAR, 112, 128), BF16),
            ((2, 7 * PAN, 128), BF16),
            ((256, 128), F32),
            ((256, 128), F32),
        ],
        [pltpu.VMEM((PAN, 384), F32)],
        flops=10**9,
        name="level2",
    )(sc, d1, d1s, f0, f1, tk, tr)
    tr = crossed(ts, 4)
    thick = gather_front(thick, 112).reshape(NEAR, FAR, 112, 128)
    (piece,) = call(
        top_kernel,
        [VMEM] * 4,
        [((248, 128), F32)],
        [pltpu.VMEM((512, 7 * PAN), F32)],
        name="top",
    )(tk, tr, thick, vw)
    pieces = lax.all_gather(piece, "cube", axis=0)
    (top,) = call(last_kernel, [VMEM], [((KEEP, KEEP * N), F32)], name="last")(pieces)
    return factors[None], top


def solution(mesh):
    in_specs = (P("cube", "front", None), P(None, "front", None), P())
    out_specs = (P("cube", None, "front", None), P("front", None))
    return jax.shard_map(
        on_device, mesh=mesh, in_specs=in_specs, out_specs=out_specs, check_vma=False
    )
```

```python
import functools

import jax
import jax.numpy as jnp
from jax import lax
from jax.experimental import pallas as pl
from jax.experimental.pallas import tpu as pltpu
from jax.sharding import PartitionSpec as P

F32 = jnp.float32
BF16 = jnp.bfloat16
HIGH = lax.Precision.HIGHEST

N = 64
FAR, NEAR = 8, 8
WIDTH = 64
KEEP = 60
PAN = 256
BLK = 32

FAR_GROUPS = [[NEAR * far + near for far in range(FAR)] for near in range(NEAR)]
NEAR_GROUPS = [[NEAR * far + near for near in range(NEAR)] for far in range(FAR)]
CORE_GROUPS = [[0, 1], [2, 3], [4, 5], [6, 7]]

VMEM = pl.BlockSpec(memory_space=pltpu.VMEM)
SMEM = pl.BlockSpec(memory_space=pltpu.SMEM)


def iota(shape, dim):
    return lax.broadcasted_iota(jnp.int32, shape, dim)


def split3(x):
    high = x.astype(BF16)
    rest = x - high.astype(F32)
    mid = rest.astype(BF16)
    low = (rest - mid.astype(F32)).astype(BF16)
    return high, mid, low


def dot(a, b, dims):
    return lax.dot_general(a, b, (dims, ((), ())), preferred_element_type=F32)


NN = ((1,), (0,))
NT = ((1,), (1,))
TN = ((0,), (0,))


def onehot_rows(row):
    return (iota((WIDTH, WIDTH), 0) == row).astype(BF16)


def compose(a, b):
    return dot(a, b, NN).astype(BF16)


def tail_table():
    return (iota((WIDTH, WIDTH), 0) + 4 == iota((WIDTH, WIDTH), 1)).astype(BF16)


def unpack(packed):
    full = jnp.concatenate([packed, pltpu.roll(packed, 64, 1)], axis=0)
    return jnp.where(iota(full.shape, 1) < WIDTH, full, 0.0)


def spread_over(x, shape):
    return jnp.broadcast_to(x, shape)


def factor(a_ref, width):
    tile = (8, 128)
    rid = iota(tile, 0)
    count = BLK // 8
    for b in range(PAN // BLK):
        j0 = b * BLK
        lo = j0 // 128 * 128
        wide = width - lo
        tiles = [a_ref[j0 + 8 * t : j0 + 8 * t + 8, lo:width] for t in range(count)]
        roots = []
        for g in range(count):
            c0 = j0 - lo + 8 * g
            cols = [
                [spread_over(tiles[t][:, c0 + k : c0 + k + 1], tile) for t in range(g, count)]
                for k in range(8)
            ]
            for i in range(8):
                pivot = spread_over(cols[i][0][i : i + 1, :], tile)
                inv = 1.0 / pivot
                r = lax.rsqrt(pivot)
                r = r * (1.5 - 0.5 * pivot * r * r)
                root = r if i == 0 else jnp.where(rid >= i, r, root)
                scale = [c * inv for c in cols[i]]
                scale[0] = jnp.where(rid > i, scale[0], 0.0)
                for k in range(i + 1, 8):
                    s = spread_over(cols[i][0][k : k + 1, :], tile)
                    cols[k] = [c - f * s for c, f in zip(cols[k], scale)]
                row = spread_over(tiles[g][i : i + 1, :], (8, wide))
                for t in range(g, count):
                    f = scale[t - g]
                    tiles[t] = jnp.concatenate(
                        [
                            tiles[t][:, q : q + 128] - f * row[:, q : q + 128]
                            for q in range(0, wide, 128)
                        ],
                        axis=1,
                    )
            roots.append(root)
        tiles = [
            jnp.concatenate([x[:, q : q + 128] * r for q in range(0, wide, 128)], axis=1)
            for x, r in zip(tiles, roots)
        ]
        rows = jnp.concatenate(tiles, axis=0)
        a_ref[j0 : j0 + BLK, lo:width] = rows
        r0 = j0 + BLK
        if r0 < PAN:
            nlo = r0 // 128 * 128
            h, m, l = split3(rows[:, nlo - lo :])
            n = PAN - nlo
            left = jnp.concatenate([h, h, m, h, l, m], axis=0)[:, :n]
            right = jnp.concatenate([h, m, h, l, h, m], axis=0)
            done = dot(left, right, TN)
            a_ref[r0:PAN, nlo:width] -= done[r0 - nlo :, :]


def own_columns(own, position):
    p = iota(own.shape, 0)
    t = iota(own.shape, 1)
    kept = jnp.where((t < 4) & (p > t * N + position), 0.0, own)
    return jnp.transpose(kept)[:WIDTH, :]


def rows_of(g_ref, part, first, count, out_ref, more=None):
    for r in range(count):
        for near in range(NEAR):
            for half in range(2):
                at = half * 12 + first + r
                got = g_ref[near // 4][part, near % 4, pl.ds(at, FAR, stride=24), :]
                if more is not None:
                    at = at + near % 4 * FAR * 24
                    got = got + more[near // 4, pl.ds(at, FAR, stride=24), :]
                out_ref[half, pl.ds(r * N + near, FAR, stride=NEAR), :] = got


def joined(r, first, last):
    return jnp.concatenate([r[0, first:last, :], r[1, first:last, :]], axis=1)


def symmetric(g):
    return jnp.where(iota(g.shape, 1) >= iota(g.shape, 0), jnp.transpose(g), g)


def leaf_kernel(
    sc, maps_s, maps_v, leaf, entries, e_ref, ent_ref, t_ref, big, inv
):
    cube = sc[3]
    chunks = 3840 // 256

    @pl.loop(0, 72)
    def _(k):
        inv[k] = -1

    @pl.loop(0, KEEP, unroll=12)
    def _(v):
        a0 = maps_s[0, v]
        a1 = maps_s[1, a0]
        a2 = maps_s[2, jnp.maximum(a1, 0)]
        code = jnp.where(a0 < 4, a0, jnp.where(a1 < 4, 4 + a1, 8 + a2))
        inv[code] = v

    t0 = onehot_rows(maps_v[0:1, :])
    t1 = compose(onehot_rows(maps_v[1:2, :]), t0)
    t2 = compose(onehot_rows(maps_v[2:3, :]), t1)
    tt = compose(tail_table(), t2)
    table = jnp.concatenate([tt, t0, t1, t2], axis=0).astype(F32)
    table = jnp.transpose(table).astype(BF16)
    table = jnp.concatenate([table, table, table], axis=0)

    pad = jnp.zeros((WIDTH - KEEP, 256), F32)
    for j in range(chunks):
        block = leaf[0, :, j * 256 : (j + 1) * 256]
        block = jnp.concatenate([block, pad], axis=0)
        parts = jnp.concatenate(split3(block), axis=0)
        turned = dot(parts, table, TN)
        big[0, j * 256 : (j + 1) * 256, :] = turned[:, 0:128]
        big[1, j * 256 : (j + 1) * 256, :] = turned[:, 128:256]

    lane = iota((N, 128), 1)
    for h in range(3):
        for k in range(2):
            pieces = []
            for side in range(2):
                v = inv[h * 4 + side * 2 + k]
                got = big[(h + 1) // 2, pl.ds(jnp.maximum(v, 0), N, stride=KEEP), :]
                if (h + 1) % 2 != side:
                    got = pltpu.roll(got, 64, 1)
                pieces.append(jnp.where(v >= 0, got, 0.0))
            e_ref[h, k * N : (k + 1) * N, :] = jnp.where(lane < WIDTH, pieces[0], pieces[1])

    half_lane = iota((N // 2, 128), 1)
    for s in range(8):
        r = jnp.bitwise_xor(s, cube)
        slot = jnp.bitwise_and(r, 1) * 4 + jnp.bitwise_and(r, 2) + jnp.right_shift(r, 2)
        for i in range(8):
            dst = pl.ds(slot * 256 + i, N // 2, stride=8)
            if s * 8 + i < KEEP:
                v = inv[12 + s * 8 + i]
                start = jnp.maximum(v, 0)
                low = big[0, pl.ds(start, N // 2, stride=KEEP), :]
                high = big[0, pl.ds(start + KEEP * N // 2, N // 2, stride=KEEP), :]
                got = jnp.where(half_lane < WIDTH, low, pltpu.roll(high, 64, 1))
                got = jnp.where(v >= 0, got, 0.0)
            else:
                got = jnp.zeros((N // 2, 128), F32)

            t_ref[dst, :] = got

    p = iota((PAN, PAN), 0)
    order = (iota((PAN, PAN), 1) == (p % N) * 4 + p // N).astype(BF16)
    for h in range(3):
        e = entries[sc[h]]
        e3 = split3(e)
        placed = dot(order, e3[0], NT) + dot(order, e3[1], NT) + dot(order, e3[2], NT)
        ent_ref[h] = jnp.concatenate([placed[:128], placed[128:]], axis=1)


def pick_kernel(sc, maps_v, e, ent, x_ref, xp_ref, send_ref):
    core = sc[5]
    x = jnp.right_shift(sc[3], 1)
    x0 = e[0, 0] + e[1, 0] + ent[0]
    x1 = e[0, 1] + e[1, 1] + jnp.where(jnp.bitwise_and(x, 1) == 0, ent[1], 0.0)
    x2 = e[0, 2] + e[1, 2] + jnp.where(x == 0, ent[2], 0.0)
    x_ref[...] = x0
    xp_ref[0], xp_ref[1] = x1, x2
    m1 = onehot_rows(maps_v[1:2, :])
    m2 = onehot_rows(maps_v[2:3, :])
    m21 = compose(m2, m1)
    eye = (iota((WIDTH, WIDTH), 0) == iota((WIDTH, WIDTH), 1)).astype(BF16)

    def first4(tables):
        four = [x.astype(F32)[:8] for x in tables]
        while len(four) < 3:
            four.append(jnp.zeros_like(four[0]))
        return jnp.concatenate(four, axis=0)

    zero = jnp.zeros((8, WIDTH), F32)
    s0 = jnp.where(core == 0, first4([eye, m1, m21]), 0.0)
    s1 = jnp.where(core == 1, first4([eye, m2]), 0.0)
    s2 = jnp.where(
        core == 1, jnp.concatenate([zero, zero, eye.astype(F32)[:8]], axis=0), 0.0
    )
    z = jnp.zeros((24, PAN), F32)
    for s, x in ((s0, x0), (s1, x1), (s2, x2)):
        full = jnp.concatenate([x, pltpu.roll(x, 64, 1)], axis=0)[:, :WIDTH]
        table = s.astype(BF16)
        h, m, l = split3(full)
        z = z + (dot(table, h, NT) + dot(table, m, NT) + dot(table, l, NT))
    rows = jnp.concatenate([z[0:4], z[8:12], z[16:20]], axis=0)
    rows = jnp.concatenate([rows[:, :128], rows[:, 128:]], axis=0)
    for k in range(FAR):
        send_ref[k] = rows


def level0_kernel(sc, maps_v, ga, gb, x, ta, tr, f_ref, v_ref, tk_ref, ts_ref, a, r):
    tk_ref[...] = ta[0:512, :] + tr[0:512, :]
    ts_ref[...] = ta[512:1024, :] + tr[512:1024, :]
    rows_of((ga, gb), 0, 0, 12, r)
    a[:, 0:256] = symmetric(joined(r, 0, 256))
    a[:, 256:768] = jnp.transpose(joined(r, 256, 768))
    a[:, 768:896] = unpack(x[...])
    factor(a, 896)
    own = a[:, 768:896]
    f_ref[...] = own_columns(own, sc[4])
    m1 = onehot_rows(maps_v[1:2, :])
    v_ref[:, 0:512] = a[:, 256:768].astype(BF16)
    moved = dot(own[:, :WIDTH].astype(BF16), m1, NT)
    v_ref[:, 512:640] = jnp.concatenate([moved, jnp.zeros_like(moved)], axis=1).astype(BF16)


def level1_kernel(
    sc, maps_v, ga, gb, xp, cross, more, v0, v0s, f_ref, d_ref, half_ref, a, r
):
    rows_of((ga, gb), 1, 0, 12, r, more)
    a[:, 0:256] = symmetric(joined(r, 0, 256))
    a[:, 256:512] = jnp.transpose(joined(r, 256, 512))
    a[:, 512:640] = unpack(xp[0] + cross[768:896, :])
    mine, other = v0[...], v0s[...]
    a[...] -= dot(mine[:, 0:256], mine, TN) + dot(other[:, 0:256], other, TN)
    factor(a, 640)
    own = a[:, 512:640]
    f_ref[...] = own_columns(own, sc[4])
    m2 = onehot_rows(maps_v[2:3, :])
    moved = [
        dot(mine[:, 512 : 512 + WIDTH], m2, NT).astype(BF16),
        dot(other[:, 512 : 512 + WIDTH], m2, NT).astype(BF16),
        dot(own[:, :WIDTH].astype(BF16), m2, NT).astype(BF16),
    ]
    cols = [mine[:, 256:512], other[:, 256:512], a[:, 256:512].astype(BF16)]
    zero = jnp.zeros((PAN, WIDTH), F32)
    right0 = [jnp.concatenate([c.astype(F32), m.astype(F32), zero], axis=1) for c, m in zip(cols, moved)]
    total = jnp.zeros((PAN, 384), F32)
    for c, right in zip(cols, right0):
        total = total + dot(c, right.astype(BF16), TN)
    d_ref[:, 0:256] = total[:, 0:256] - symmetric(joined(r, 512, 768))
    own2 = unpack(xp[1] + cross[896:1024, :])
    total = total[:, 256:384] - own2
    d_ref[:, 256:384] = jnp.concatenate(
        [total[:, :WIDTH], moved[0].astype(F32)], axis=1
    )
    d_ref[:, 384:512] = jnp.concatenate(
        [moved[1].astype(F32), moved[2].astype(F32)], axis=1
    )
    first = pl.multiple_of(sc[5] * 128, 128)
    half_ref[...] = d_ref[pl.ds(first, 128), :]


def level2_kernel(sc, d, ds, f0, f1, f_ref, send_ref, vw_ref, a):
    sib = jnp.concatenate([ds[0], ds[1]], axis=0)
    mine = d[...]
    sub = mine[:, 0:384] + sib[:, 0:384]
    a[:, 0:256] = -sub[:, 0:256]
    a[:, 256:384] = jnp.where(iota((PAN, 128), 1) < WIDTH, -sub[:, 256:384], 0.0)
    factor(a, 384)
    own = a[:, 256:384]
    f_ref[0] = f0[...]
    f_ref[1] = f1[...]
    f_ref[2] = own_columns(own, sc[4])
    pieces = [
        m[:, first : first + WIDTH].astype(BF16)
        for m in (mine, sib)
        for first in (320, 384, 448)
    ]
    pieces.append(own[:, :WIDTH].astype(BF16))
    first = 4 + 8 * sc[3]
    pick = (iota((8, WIDTH), 0) + first == iota((8, WIDTH), 1)).astype(BF16)
    thick = jnp.concatenate([dot(pick, v, NT) for v in pieces], axis=0)
    thick = jnp.concatenate([thick[:, :128], thick[:, 128:]], axis=0).astype(BF16)
    for k in range(FAR):
        send_ref[k] = thick
    src = iota((WIDTH, 128), 0)
    dst = iota((WIDTH, 128), 1)
    low = (src == dst + 4).astype(BF16)
    low = jnp.where(dst < KEEP, low, jnp.zeros_like(low))
    high = ((src == dst - 60) & (dst >= WIDTH)).astype(BF16)
    for n, v in enumerate(pieces):
        vw_ref[0, n * PAN : (n + 1) * PAN, :] = dot(v, low, NN).astype(BF16)
        vw_ref[1, n * PAN : (n + 1) * PAN, :] = dot(v, high, NN).astype(BF16)


def top_kernel(tk, tr, got, vw, out, big):
    for near in range(NEAR):
        for far in range(FAR):
            block = got[near, far].astype(F32)
            d = far * NEAR + near
            for n in range(7):
                for half in range(2):
                    first = half * 56 + n * 8
                    big[d * 8 : d * 8 + 8, (n * 2 + half) * 128 : (n * 2 + half + 1) * 128] = (
                        block[first : first + 8, :]
                    )
    low = dot(big[0:256, :].astype(BF16), vw[0], NN)
    high = dot(big[256:512, :].astype(BF16), vw[1], NN)
    piece = tk[...] + tr[...] - (low + high)
    last = piece[248:256, :]
    lane = iota((8, 128), 1)
    for t in range(31):
        rows = piece[8 * t : 8 * t + 8, :]
        if t < 16:
            one = pltpu.roll(last, (60 - 8 * t) % 128, 1)
            two = pltpu.roll(last, (120 - 8 * t) % 128, 1)
            rows = jnp.where(
                lane >= 124, two, jnp.where((lane >= 60) & (lane < 64), one, rows)
            )
        out[8 * t : 8 * t + 8, :] = rows


def last_kernel(t, out):
    lane = iota((8, 128), 1)
    ends = []
    for s in range(8):
        end = jnp.zeros((8, 128), F32)
        for k in range(16):
            rows = t[s, 8 * k : 8 * k + 8, :]
            one = pltpu.roll(rows, (8 * k - 60) % 128, 1)
            two = pltpu.roll(rows, (8 * k - 120) % 128, 1)
            end = jnp.where(lane // 4 == 2 * k, one, jnp.where(lane // 4 == 2 * k + 1, two, end))
        ends.append(end)
    for d in range(N // 2):
        if d < N // 2 - 1:
            block = jnp.concatenate([t[s, d * 8 : d * 8 + 8, :] for s in range(8)], axis=0)
        else:
            block = jnp.concatenate(ends, axis=0)
        turned = jnp.transpose(block)
        out[:, d * KEEP : (d + 1) * KEEP] = turned[0:KEEP, 0:KEEP]
        d2 = d + N // 2
        out[:, d2 * KEEP : (d2 + 1) * KEEP] = turned[WIDTH : WIDTH + KEEP, 0:KEEP]


def call(kernel, specs, outs, scratch=(), flops=10**8, name=None):
    return pl.pallas_call(
        kernel,
        in_specs=specs,
        out_specs=[VMEM] * len(outs),
        out_shape=[jax.ShapeDtypeStruct(s, t) for s, t in outs],
        scratch_shapes=list(scratch),
        compiler_params=pltpu.CompilerParams(vmem_limit_bytes=48 * 2**20),
        cost_estimate=pl.CostEstimate(flops=flops, bytes_accessed=4 * 10**6, transcendentals=0),
        name=name,
    )


def crossed(value, mask):
    return lax.ppermute(value, "cube", [(c, c ^ mask) for c in range(8)])


def spread(value, axis_groups):
    return lax.all_to_all(value, "front", 0, 0, axis_index_groups=axis_groups, tiled=True)


def far_gather(sent, rows):
    return spread(sent.reshape(FAR * rows, sent.shape[-1]), FAR_GROUPS)


def near_copies(got):
    return jnp.broadcast_to(got[None], (NEAR,) + got.shape)


def near_gather(copies):
    shape = copies.shape
    return spread(copies.reshape(shape[0] * shape[1], shape[2]), NEAR_GROUPS).reshape(shape)


def gather_front(sent, rows):
    return near_gather(near_copies(far_gather(sent, rows)))


def on_device(leaf_blocks, front_entries, child_maps):
    position = lax.axis_index("front")
    cube = lax.axis_index("cube")
    core = cube & 1
    nodes = [jnp.right_shift(cube + 8, h + 1) for h in range(3)]
    sides = [jnp.right_shift(cube, h) & 1 for h in range(3)]
    sc = jnp.stack(
        [n - 1 for n in nodes] + [cube, position, core, jnp.right_shift(cube, 2), cube * 0]
    ).astype(jnp.int32)
    picked = [
        lax.dynamic_slice(child_maps, (n - 1, s, 0), (1, 1, KEEP)).reshape(KEEP)
        for n, s in zip(nodes, sides)
    ]
    none = jnp.full((4,), -1, jnp.int32)
    maps = jnp.stack(
        [
            jnp.concatenate([picked[0], none]),
            jnp.concatenate([none, picked[1]]),
            jnp.concatenate([none, picked[2]]),
        ]
    )

    e, ent, t = call(
        leaf_kernel,
        [SMEM, SMEM, VMEM, VMEM, VMEM],
        [((3, 128, 128), F32), ((3, 128, 128), F32), ((2048, 128), F32)],
        [
            pltpu.VMEM((2, 3840, 128), F32),
            pltpu.SMEM((128,), jnp.int32),
        ],
        name="leaf",
    )(sc, maps, maps, leaf_blocks, front_entries)

    both = lax.all_gather(e, "cube", axis_index_groups=CORE_GROUPS, axis=0)
    x, xp, sent = call(
        pick_kernel,
        [SMEM] + [VMEM] * 3,
        [((128, 128), F32), ((2, 128, 128), F32), ((FAR, 24, 128), F32)],
        name="pick",
    )(sc, maps, both, ent)
    g = gather_front(sent, 24)
    ga, gb = [
        lax.all_gather(part, "cube", axis_index_groups=CORE_GROUPS, axis=0)
        for part in (g[:4], g[4:])
    ]

    mine = jnp.where(core == 0, ga[1], gb[1]).reshape(768, 128)
    cross = crossed(jnp.concatenate([mine, xp.reshape(256, 128)], axis=0), 2)

    tr = crossed(t[1024:], 1)
    f0, v0, tk, ts = call(
        level0_kernel,
        [SMEM] + [VMEM] * 6,
        [((WIDTH, PAN), F32), ((PAN, 640), BF16), ((512, 128), F32), ((512, 128), F32)],
        [pltpu.VMEM((PAN, 896), F32), pltpu.VMEM((2, 768, 128), F32)],
        flops=10**9,
        name="level0",
    )(sc, maps, ga, gb, x, t, tr)
    v0s = crossed(v0, 2)
    more = lax.all_gather(cross[:768], "cube", axis_index_groups=CORE_GROUPS, axis=0)
    f1, d1, half = call(
        level1_kernel,
        [SMEM] + [VMEM] * 8,
        [((WIDTH, PAN), F32), ((PAN, 512), F32), ((128, 512), F32)],
        [pltpu.VMEM((PAN, 640), F32), pltpu.VMEM((2, 768, 128), F32)],
        flops=10**9,
        name="level1",
    )(sc, maps, ga, gb, xp, cross, more, v0, v0s)
    d1s = lax.all_gather(crossed(half, 4), "cube", axis_index_groups=CORE_GROUPS, axis=0)
    factors, thick, vw = call(
        level2_kernel,
        [SMEM] + [VMEM] * 4,
        [
            ((3, WIDTH, PAN), F32),
            ((FAR, 112, 128), BF16),
            ((2, 7 * PAN, 128), BF16),
        ],
        [pltpu.VMEM((PAN, 384), F32)],
        flops=10**9,
        name="level2",
    )(sc, d1, d1s, f0, f1)
    thick = far_gather(thick, 112)
    thick, ts = lax.optimization_barrier((near_copies(thick), ts))
    thick = near_gather(thick).reshape(NEAR, FAR, 112, 128)
    tr = crossed(ts, 2)
    tk, ts = tk[:256] + tr[:256], tk[256:] + tr[256:]
    tr = crossed(ts, 4)
    (piece,) = call(
        top_kernel,
        [VMEM] * 4,
        [((248, 128), F32)],
        [pltpu.VMEM((512, 7 * PAN), F32)],
        name="top",
    )(tk, tr, thick, vw)
    pieces = lax.all_gather(piece, "cube", axis=0)
    (top,) = call(last_kernel, [VMEM], [((KEEP, KEEP * N), F32)], name="last")(pieces)
    return factors[None], top


def solution(mesh):
    in_specs = (P("cube", "front", None), P(None, "front", None), P())
    out_specs = (P("cube", None, "front", None), P("front", None))
    return jax.shard_map(
        on_device, mesh=mesh, in_specs=in_specs, out_specs=out_specs, check_vma=False
    )
```

```python
import functools

import jax
import jax.numpy as jnp
from jax import lax
from jax.experimental import pallas as pl
from jax.experimental.pallas import tpu as pltpu
from jax.sharding import PartitionSpec as P

F32 = jnp.float32
BF16 = jnp.bfloat16
HIGH = lax.Precision.HIGHEST

N = 64
FAR, NEAR = 8, 8
WIDTH = 64
KEEP = 60
PAN = 256
BLK = 32

FAR_GROUPS = [[NEAR * far + near for far in range(FAR)] for near in range(NEAR)]
NEAR_GROUPS = [[NEAR * far + near for near in range(NEAR)] for far in range(FAR)]
CORE_GROUPS = [[0, 1], [2, 3], [4, 5], [6, 7]]

VMEM = pl.BlockSpec(memory_space=pltpu.VMEM)
SMEM = pl.BlockSpec(memory_space=pltpu.SMEM)


def iota(shape, dim):
    return lax.broadcasted_iota(jnp.int32, shape, dim)


def split3(x):
    high = x.astype(BF16)
    rest = x - high.astype(F32)
    mid = rest.astype(BF16)
    low = (rest - mid.astype(F32)).astype(BF16)
    return high, mid, low


def dot(a, b, dims):
    return lax.dot_general(a, b, (dims, ((), ())), preferred_element_type=F32)


NN = ((1,), (0,))
NT = ((1,), (1,))
TN = ((0,), (0,))


def onehot_rows(row):
    return (iota((WIDTH, WIDTH), 0) == row).astype(BF16)


def compose(a, b):
    return dot(a, b, NN).astype(BF16)


def tail_table():
    return (iota((WIDTH, WIDTH), 0) + 4 == iota((WIDTH, WIDTH), 1)).astype(BF16)


def unpack(packed):
    full = jnp.concatenate([packed, pltpu.roll(packed, 64, 1)], axis=0)
    return jnp.where(iota(full.shape, 1) < WIDTH, full, 0.0)


def spread_over(x, shape):
    return jnp.broadcast_to(x, shape)


def factor(a_ref, width):
    tile = (8, 128)
    rid = iota(tile, 0)
    count = BLK // 8
    for b in range(PAN // BLK):
        j0 = b * BLK
        lo = j0 // 128 * 128
        wide = width - lo
        tiles = [a_ref[j0 + 8 * t : j0 + 8 * t + 8, lo:width] for t in range(count)]
        roots = []
        for g in range(count):
            c0 = j0 - lo + 8 * g
            cols = [
                [spread_over(tiles[t][:, c0 + k : c0 + k + 1], tile) for t in range(g, count)]
                for k in range(8)
            ]
            for i in range(8):
                pivot = spread_over(cols[i][0][i : i + 1, :], tile)
                inv = 1.0 / pivot
                r = lax.rsqrt(pivot)
                r = r * (1.5 - 0.5 * pivot * r * r)
                root = r if i == 0 else jnp.where(rid >= i, r, root)
                scale = [c * inv for c in cols[i]]
                scale[0] = jnp.where(rid > i, scale[0], 0.0)
                for k in range(i + 1, 8):
                    s = spread_over(cols[i][0][k : k + 1, :], tile)
                    cols[k] = [c - f * s for c, f in zip(cols[k], scale)]
                row = spread_over(tiles[g][i : i + 1, :], (8, wide))
                for t in range(g, count):
                    f = scale[t - g]
                    tiles[t] = jnp.concatenate(
                        [
                            tiles[t][:, q : q + 128] - f * row[:, q : q + 128]
                            for q in range(0, wide, 128)
                        ],
                        axis=1,
                    )
            roots.append(root)
        tiles = [
            jnp.concatenate([x[:, q : q + 128] * r for q in range(0, wide, 128)], axis=1)
            for x, r in zip(tiles, roots)
        ]
        rows = jnp.concatenate(tiles, axis=0)
        a_ref[j0 : j0 + BLK, lo:width] = rows
        r0 = j0 + BLK
        if r0 < PAN:
            nlo = r0 // 128 * 128
            h, m, l = split3(rows[:, nlo - lo :])
            n = PAN - nlo
            left = jnp.concatenate([h, h, m, h, l, m], axis=0)[:, :n]
            right = jnp.concatenate([h, m, h, l, h, m], axis=0)
            done = dot(left, right, TN)
            a_ref[r0:PAN, nlo:width] -= done[r0 - nlo :, :]


def own_columns(own, position):
    p = iota(own.shape, 0)
    t = iota(own.shape, 1)
    kept = jnp.where((t < 4) & (p > t * N + position), 0.0, own)
    return jnp.transpose(kept)[:WIDTH, :]


def rows_of(g_ref, part, first, count, out_ref, more=None):
    for r in range(count):
        for near in range(NEAR):
            for half in range(2):
                at = half * 12 + first + r
                got = g_ref[near // 4][part, near % 4, pl.ds(at, FAR, stride=24), :]
                if more is not None:
                    at = at + near % 4 * FAR * 24
                    got = got + more[near // 4, pl.ds(at, FAR, stride=24), :]
                out_ref[half, pl.ds(r * N + near, FAR, stride=NEAR), :] = got


def joined(r, first, last):
    return jnp.concatenate([r[0, first:last, :], r[1, first:last, :]], axis=1)


def symmetric(g):
    return jnp.where(iota(g.shape, 1) >= iota(g.shape, 0), jnp.transpose(g), g)


def leaf_kernel(
    sc, child_s, child_v, leaf, entries, e_ref, ent_ref, t_ref, maps_ref, big, inv
):
    cube = sc[3]
    chunks = 3840 // 256
    sides = [jnp.bitwise_and(jnp.right_shift(cube, h), 1) for h in range(3)]

    @pl.loop(0, 72)
    def _(k):
        inv[k] = -1

    @pl.loop(0, KEEP, unroll=12)
    def _(v):
        a0 = child_s[sc[0], sides[0], v]
        a1 = child_s[sc[1], sides[1], jnp.maximum(a0 - 4, 0)]
        a2 = child_s[sc[2], sides[2], jnp.maximum(a1 - 4, 0)]
        code = jnp.where(a0 < 4, a0, jnp.where(a1 < 4, 4 + a1, 8 + a2))
        inv[code] = v

    none = jnp.full((1, 4), -1, jnp.int32)
    rows = []
    for h in range(3):
        two = child_v[sc[h]]
        row = jnp.where(sides[h] == 0, two[0:1, :], two[1:2, :])
        rows.append(jnp.concatenate([row, none] if h == 0 else [none, row], axis=1))
        maps_ref[h : h + 1, :] = rows[h]
    t0 = onehot_rows(rows[0])
    t1 = compose(onehot_rows(rows[1]), t0)
    t2 = compose(onehot_rows(rows[2]), t1)
    tt = compose(tail_table(), t2)
    table = jnp.concatenate([tt, t0, t1, t2], axis=0).astype(F32)
    table = jnp.transpose(table).astype(BF16)
    table = jnp.concatenate([table, table, table], axis=0)

    pad = jnp.zeros((WIDTH - KEEP, 256), F32)
    for j in range(chunks):
        block = jnp.concatenate(
            [leaf[pl.ds(2 * j + k, KEEP, stride=30), :] for k in range(2)], axis=1
        )
        block = jnp.concatenate([block, pad], axis=0)
        parts = jnp.concatenate(split3(block), axis=0)
        turned = dot(parts, table, TN)
        big[0, j * 256 : (j + 1) * 256, :] = turned[:, 0:128]
        big[1, j * 256 : (j + 1) * 256, :] = turned[:, 128:256]

    lane = iota((N, 128), 1)
    for h in range(3):
        for k in range(2):
            pieces = []
            for side in range(2):
                v = inv[h * 4 + side * 2 + k]
                got = big[(h + 1) // 2, pl.ds(jnp.maximum(v, 0), N, stride=KEEP), :]
                if (h + 1) % 2 != side:
                    got = pltpu.roll(got, 64, 1)
                pieces.append(jnp.where(v >= 0, got, 0.0))
            e_ref[h, k * N : (k + 1) * N, :] = jnp.where(lane < WIDTH, pieces[0], pieces[1])

    half_lane = iota((N // 2, 128), 1)
    for s in range(8):
        r = jnp.bitwise_xor(s, cube)
        slot = jnp.bitwise_and(r, 1) * 4 + jnp.bitwise_and(r, 2) + jnp.right_shift(r, 2)
        for i in range(8):
            dst = pl.ds(slot * 256 + i, N // 2, stride=8)
            if s * 8 + i < KEEP:
                v = inv[12 + s * 8 + i]
                start = jnp.maximum(v, 0)
                low = big[0, pl.ds(start, N // 2, stride=KEEP), :]
                high = big[0, pl.ds(start + KEEP * N // 2, N // 2, stride=KEEP), :]
                got = jnp.where(half_lane < WIDTH, low, pltpu.roll(high, 64, 1))
                got = jnp.where(v >= 0, got, 0.0)
            else:
                got = jnp.zeros((N // 2, 128), F32)

            t_ref[dst, :] = got

    p = iota((PAN, PAN), 0)
    order = (iota((PAN, PAN), 1) == (p % N) * 4 + p // N).astype(BF16)
    for h in range(3):
        e = entries[sc[h]]
        e3 = split3(e)
        placed = dot(order, e3[0], NT) + dot(order, e3[1], NT) + dot(order, e3[2], NT)
        ent_ref[h] = jnp.concatenate([placed[:128], placed[128:]], axis=1)


def pick_kernel(sc, maps_v, e, ent, x_ref, xp_ref, send_ref):
    core = sc[5]
    x = jnp.right_shift(sc[3], 1)
    x0 = e[0, 0] + e[1, 0] + ent[0]
    x1 = e[0, 1] + e[1, 1] + jnp.where(jnp.bitwise_and(x, 1) == 0, ent[1], 0.0)
    x2 = e[0, 2] + e[1, 2] + jnp.where(x == 0, ent[2], 0.0)
    x_ref[...] = x0
    xp_ref[0], xp_ref[1] = x1, x2
    m1 = onehot_rows(maps_v[1:2, :])
    m2 = onehot_rows(maps_v[2:3, :])
    m21 = compose(m2, m1)
    eye = (iota((WIDTH, WIDTH), 0) == iota((WIDTH, WIDTH), 1)).astype(BF16)

    def first4(tables):
        four = [x.astype(F32)[:8] for x in tables]
        while len(four) < 3:
            four.append(jnp.zeros_like(four[0]))
        return jnp.concatenate(four, axis=0)

    zero = jnp.zeros((8, WIDTH), F32)
    s0 = jnp.where(core == 0, first4([eye, m1, m21]), 0.0)
    s1 = jnp.where(core == 1, first4([eye, m2]), 0.0)
    s2 = jnp.where(
        core == 1, jnp.concatenate([zero, zero, eye.astype(F32)[:8]], axis=0), 0.0
    )
    z = jnp.zeros((24, PAN), F32)
    for s, x in ((s0, x0), (s1, x1), (s2, x2)):
        full = jnp.concatenate([x, pltpu.roll(x, 64, 1)], axis=0)[:, :WIDTH]
        table = s.astype(BF16)
        h, m, l = split3(full)
        z = z + (dot(table, h, NT) + dot(table, m, NT) + dot(table, l, NT))
    rows = jnp.concatenate([z[0:4], z[8:12], z[16:20]], axis=0)
    rows = jnp.concatenate([rows[:, :128], rows[:, 128:]], axis=0)
    for k in range(FAR):
        send_ref[k] = rows


def level0_kernel(sc, maps_v, ga, gb, x, ta, tr, f_ref, v_ref, tk_ref, ts_ref, a, r):
    tk_ref[...] = ta[0:512, :] + tr[0:512, :]
    ts_ref[...] = ta[512:1024, :] + tr[512:1024, :]
    rows_of((ga, gb), 0, 0, 12, r)
    a[:, 0:256] = symmetric(joined(r, 0, 256))
    a[:, 256:768] = jnp.transpose(joined(r, 256, 768))
    a[:, 768:896] = unpack(x[...])
    factor(a, 896)
    own = a[:, 768:896]
    f_ref[...] = own_columns(own, sc[4])
    m1 = onehot_rows(maps_v[1:2, :])
    v_ref[:, 0:512] = a[:, 256:768].astype(BF16)
    moved = dot(own[:, :WIDTH].astype(BF16), m1, NT)
    v_ref[:, 512:640] = jnp.concatenate([moved, jnp.zeros_like(moved)], axis=1).astype(BF16)


def level1_kernel(
    sc, maps_v, ga, gb, xp, cross, more, v0, v0s, f_ref, d_ref, half_ref, a, r
):
    rows_of((ga, gb), 1, 0, 12, r, more)
    a[:, 0:256] = symmetric(joined(r, 0, 256))
    a[:, 256:512] = jnp.transpose(joined(r, 256, 512))
    a[:, 512:640] = unpack(xp[0] + cross[768:896, :])
    mine, other = v0[...], v0s[...]
    a[...] -= dot(mine[:, 0:256], mine, TN) + dot(other[:, 0:256], other, TN)
    factor(a, 640)
    own = a[:, 512:640]
    f_ref[...] = own_columns(own, sc[4])
    m2 = onehot_rows(maps_v[2:3, :])
    moved = [
        dot(mine[:, 512 : 512 + WIDTH], m2, NT).astype(BF16),
        dot(other[:, 512 : 512 + WIDTH], m2, NT).astype(BF16),
        dot(own[:, :WIDTH].astype(BF16), m2, NT).astype(BF16),
    ]
    cols = [mine[:, 256:512], other[:, 256:512], a[:, 256:512].astype(BF16)]
    zero = jnp.zeros((PAN, WIDTH), F32)
    right0 = [jnp.concatenate([c.astype(F32), m.astype(F32), zero], axis=1) for c, m in zip(cols, moved)]
    total = jnp.zeros((PAN, 384), F32)
    for c, right in zip(cols, right0):
        total = total + dot(c, right.astype(BF16), TN)
    d_ref[:, 0:256] = total[:, 0:256] - symmetric(joined(r, 512, 768))
    own2 = unpack(xp[1] + cross[896:1024, :])
    total = total[:, 256:384] - own2
    d_ref[:, 256:384] = jnp.concatenate(
        [total[:, :WIDTH], moved[0].astype(F32)], axis=1
    )
    d_ref[:, 384:512] = jnp.concatenate(
        [moved[1].astype(F32), moved[2].astype(F32)], axis=1
    )
    first = pl.multiple_of(sc[5] * 128, 128)
    half_ref[...] = d_ref[pl.ds(first, 128), :]


def level2_kernel(sc, d, ds, f0, f1, f_ref, send_ref, vw_ref, a):
    sib = jnp.concatenate([ds[0], ds[1]], axis=0)
    mine = d[...]
    sub = mine[:, 0:384] + sib[:, 0:384]
    a[:, 0:256] = -sub[:, 0:256]
    a[:, 256:384] = jnp.where(iota((PAN, 128), 1) < WIDTH, -sub[:, 256:384], 0.0)
    factor(a, 384)
    own = a[:, 256:384]
    f_ref[0] = f0[...]
    f_ref[1] = f1[...]
    f_ref[2] = own_columns(own, sc[4])
    pieces = [
        m[:, first : first + WIDTH].astype(BF16)
        for m in (mine, sib)
        for first in (320, 384, 448)
    ]
    pieces.append(own[:, :WIDTH].astype(BF16))
    first = 4 + 8 * sc[3]
    pick = (iota((8, WIDTH), 0) + first == iota((8, WIDTH), 1)).astype(BF16)
    thick = jnp.concatenate([dot(pick, v, NT) for v in pieces], axis=0)
    thick = jnp.concatenate([thick[:, :128], thick[:, 128:]], axis=0).astype(BF16)
    for k in range(FAR):
        send_ref[k] = thick
    src = iota((WIDTH, 128), 0)
    dst = iota((WIDTH, 128), 1)
    low = (src == dst + 4).astype(BF16)
    low = jnp.where(dst < KEEP, low, jnp.zeros_like(low))
    high = ((src == dst - 60) & (dst >= WIDTH)).astype(BF16)
    for n, v in enumerate(pieces):
        vw_ref[0, n * PAN : (n + 1) * PAN, :] = dot(v, low, NN).astype(BF16)
        vw_ref[1, n * PAN : (n + 1) * PAN, :] = dot(v, high, NN).astype(BF16)


def top_kernel(tk, tr, got, vw, out, big):
    for near in range(NEAR):
        for far in range(FAR):
            block = got[near, far].astype(F32)
            d = far * NEAR + near
            for n in range(7):
                for half in range(2):
                    first = half * 56 + n * 8
                    big[d * 8 : d * 8 + 8, (n * 2 + half) * 128 : (n * 2 + half + 1) * 128] = (
                        block[first : first + 8, :]
                    )
    low = dot(big[0:256, :].astype(BF16), vw[0], NN)
    high = dot(big[256:512, :].astype(BF16), vw[1], NN)
    piece = tk[...] + tr[...] - (low + high)
    last = piece[248:256, :]
    lane = iota((8, 128), 1)
    for t in range(31):
        rows = piece[8 * t : 8 * t + 8, :]
        if t < 16:
            one = pltpu.roll(last, (60 - 8 * t) % 128, 1)
            two = pltpu.roll(last, (120 - 8 * t) % 128, 1)
            rows = jnp.where(
                lane >= 124, two, jnp.where((lane >= 60) & (lane < 64), one, rows)
            )
        out[8 * t : 8 * t + 8, :] = rows


def last_kernel(t, out):
    lane = iota((8, 128), 1)
    ends = []
    for s in range(8):
        end = jnp.zeros((8, 128), F32)
        for k in range(16):
            rows = t[s, 8 * k : 8 * k + 8, :]
            one = pltpu.roll(rows, (8 * k - 60) % 128, 1)
            two = pltpu.roll(rows, (8 * k - 120) % 128, 1)
            end = jnp.where(lane // 4 == 2 * k, one, jnp.where(lane // 4 == 2 * k + 1, two, end))
        ends.append(end)
    for d in range(N // 2):
        if d < N // 2 - 1:
            block = jnp.concatenate([t[s, d * 8 : d * 8 + 8, :] for s in range(8)], axis=0)
        else:
            block = jnp.concatenate(ends, axis=0)
        turned = jnp.transpose(block)
        out[:, d * KEEP : (d + 1) * KEEP] = turned[0:KEEP, 0:KEEP]
        d2 = d + N // 2
        out[:, d2 * KEEP : (d2 + 1) * KEEP] = turned[WIDTH : WIDTH + KEEP, 0:KEEP]


def call(kernel, specs, outs, scratch=(), flops=10**8, name=None):
    return pl.pallas_call(
        kernel,
        in_specs=specs,
        out_specs=[VMEM] * len(outs),
        out_shape=[jax.ShapeDtypeStruct(s, t) for s, t in outs],
        scratch_shapes=list(scratch),
        compiler_params=pltpu.CompilerParams(vmem_limit_bytes=48 * 2**20),
        cost_estimate=pl.CostEstimate(flops=flops, bytes_accessed=4 * 10**6, transcendentals=0),
        name=name,
    )


def crossed(value, mask):
    return lax.ppermute(value, "cube", [(c, c ^ mask) for c in range(8)])


def spread(value, axis_groups):
    return lax.all_to_all(value, "front", 0, 0, axis_index_groups=axis_groups, tiled=True)


def far_gather(sent, rows):
    return spread(sent.reshape(FAR * rows, sent.shape[-1]), FAR_GROUPS)


def near_copies(got):
    return jnp.broadcast_to(got[None], (NEAR,) + got.shape)


def near_gather(copies):
    shape = copies.shape
    return spread(copies.reshape(shape[0] * shape[1], shape[2]), NEAR_GROUPS).reshape(shape)


def gather_front(sent, rows):
    return near_gather(near_copies(far_gather(sent, rows)))


def on_device(leaf_blocks, front_entries, child_maps):
    position = lax.axis_index("front")
    cube = lax.axis_index("cube")
    core = cube & 1
    nodes = [jnp.right_shift(cube + 8, h + 1) for h in range(3)]
    sc = jnp.stack(
        [n - 1 for n in nodes] + [cube, position, core, jnp.right_shift(cube, 2), cube * 0]
    ).astype(jnp.int32)
    e, ent, t, maps = call(
        leaf_kernel,
        [SMEM, SMEM, VMEM, VMEM, VMEM],
        [
            ((3, 128, 128), F32),
            ((3, 128, 128), F32),
            ((2048, 128), F32),
            ((3, WIDTH), jnp.int32),
        ],
        [
            pltpu.VMEM((2, 3840, 128), F32),
            pltpu.SMEM((128,), jnp.int32),
        ],
        name="leaf",
    )(sc, child_maps, child_maps, leaf_blocks.reshape(KEEP * 30, 128), front_entries)

    both = lax.all_gather(e, "cube", axis_index_groups=CORE_GROUPS, axis=0)
    x, xp, sent = call(
        pick_kernel,
        [SMEM] + [VMEM] * 3,
        [((128, 128), F32), ((2, 128, 128), F32), ((FAR, 24, 128), F32)],
        name="pick",
    )(sc, maps, both, ent)
    g = gather_front(sent, 24)
    ga, gb = [
        lax.all_gather(part, "cube", axis_index_groups=CORE_GROUPS, axis=0)
        for part in (g[:4], g[4:])
    ]

    mine = jnp.where(core == 0, ga[1], gb[1]).reshape(768, 128)
    cross = crossed(jnp.concatenate([mine, xp.reshape(256, 128)], axis=0), 2)

    tr = crossed(t[1024:], 1)
    f0, v0, tk, ts = call(
        level0_kernel,
        [SMEM] + [VMEM] * 6,
        [((WIDTH, PAN), F32), ((PAN, 640), BF16), ((512, 128), F32), ((512, 128), F32)],
        [pltpu.VMEM((PAN, 896), F32), pltpu.VMEM((2, 768, 128), F32)],
        flops=10**9,
        name="level0",
    )(sc, maps, ga, gb, x, t, tr)
    v0s = crossed(v0, 2)
    more = lax.all_gather(cross[:768], "cube", axis_index_groups=CORE_GROUPS, axis=0)
    f1, d1, half = call(
        level1_kernel,
        [SMEM] + [VMEM] * 8,
        [((WIDTH, PAN), F32), ((PAN, 512), F32), ((128, 512), F32)],
        [pltpu.VMEM((PAN, 640), F32), pltpu.VMEM((2, 768, 128), F32)],
        flops=10**9,
        name="level1",
    )(sc, maps, ga, gb, xp, cross, more, v0, v0s)
    d1s = lax.all_gather(crossed(half, 4), "cube", axis_index_groups=CORE_GROUPS, axis=0)
    factors, thick, vw = call(
        level2_kernel,
        [SMEM] + [VMEM] * 4,
        [
            ((3, WIDTH, PAN), F32),
            ((FAR, 112, 128), BF16),
            ((2, 7 * PAN, 128), BF16),
        ],
        [pltpu.VMEM((PAN, 384), F32)],
        flops=10**9,
        name="level2",
    )(sc, d1, d1s, f0, f1)
    thick = far_gather(thick, 112)
    thick, ts = lax.optimization_barrier((near_copies(thick), ts))
    thick = near_gather(thick).reshape(NEAR, FAR, 112, 128)
    tr = crossed(ts, 2)
    tk, ts = tk[:256] + tr[:256], tk[256:] + tr[256:]
    tr = crossed(ts, 4)
    (piece,) = call(
        top_kernel,
        [VMEM] * 4,
        [((248, 128), F32)],
        [pltpu.VMEM((512, 7 * PAN), F32)],
        name="top",
    )(tk, tr, thick, vw)
    pieces = lax.all_gather(piece, "cube", axis=0)
    (top,) = call(last_kernel, [VMEM], [((KEEP, KEEP * N), F32)], name="last")(pieces)
    return factors[None], top


def solution(mesh):
    in_specs = (P("cube", "front", None), P(None, "front", None), P())
    out_specs = (P("cube", None, "front", None), P("front", None))
    return jax.shard_map(
        on_device, mesh=mesh, in_specs=in_specs, out_specs=out_specs, check_vma=False
    )
```
